256 devices in a mesh: dp: 64 (over y, x, z_lo), feat: 4 (over z_hi, core).
Axes of the slice: x: 4, y: 4, z: 8 (z_hi: 2, z_lo: 4; z = z_hi * 4 + z_lo), core: 2. Of those that a mesh axis runs over, the one named last changes fastest.
Arguments:
- frames: bfloat16 [448, 262144], P('feat', 'dp'), may hold values from -4.5 to 4.5
- residual: float32 [148, 262144], P('feat', 'dp'), may hold values from -6 to 6
- coefficients: float32 [148, 262144], P('feat', 'dp'), may hold values from -6 to 6
- block_index: int32 [2, 512], replicated, may hold values from 0 to 262143, as said below
Outputs:
- residual_out: float32 [148, 262144], P('feat', 'dp')
- coefficients_out: float32 [148, 262144], P('feat', 'dp')
The draws below stay inside these ranges and needn't reach their ends.
Inputs may be any that keep to these rules, and one draw needn't show every extreme that they name: `block_index`: the 512 indices of one step are distinct.
All inputs are finite; a program needn't handle non-finite values.
Results may differ from the reference program's by a relative error of at most 0.0003.
Values may be sent and summed in bfloat16 or wider, within the bound.
No kernel may reach another device: no remote copies, remote signals or barrier semaphores. Data moves between devices by JAX's collectives and lax.ppermute only.
A program may use at most 64 MiB of HBM per device.

```python
import jax
import jax.numpy as jnp
from jax import lax

D = 448
C = 148
BLOCK = 512
STEPS = 2
ROWS_DEV = 4096
TOTAL = 262144
N_DP = 64


def manifold_frames(key, latent_count, half_width, noise):
    mixing_key, point_key = jax.random.split(key)
    mixing = jax.random.uniform(mixing_key, (D, latent_count), jnp.float32, -half_width, half_width)
    points = jax.random.uniform(point_key, (latent_count, TOTAL), jnp.float32, -1.0, 1.0)
    smooth = jnp.zeros((D, TOTAL), jnp.float32)
    for index in range(latent_count):
        smooth = smooth + mixing[:, index:index + 1] * points[index:index + 1, :]
    return smooth + noise


def draw_frames(key, part):
    key = jax.random.fold_in(key, 11)
    shape_key, noise_key = jax.random.split(key)
    noise = jnp.clip(0.1 * jax.random.normal(noise_key, (D, TOTAL), jnp.float32), -0.3, 0.3)
    result = manifold_frames(shape_key, 6, 0.675, noise)
    return result.astype(jnp.bfloat16)


def draw_block_index(key, part):
    key = jax.random.fold_in(key, 7)
    result = []
    for step in range(STEPS):
        step_key = jax.random.fold_in(key, step)
        first_key, second_key = jax.random.split(step_key)
        inner = jax.random.permutation(first_key, TOTAL - 2)[:BLOCK - 2].astype(jnp.int32) + 1
        ends = jnp.array([0, TOTAL - 1], dtype=jnp.int32)
        whole = jnp.concatenate([inner, ends])
        order = jax.random.permutation(second_key, BLOCK)
        result.append(whole[order])
    return jnp.stack(result).astype(jnp.int32)


def levels(stream_key, dims, cuts, low, largest):
    factor_of = 1.0
    for axis_at, parts in cuts:
        steps = jax.random.uniform(jax.random.fold_in(jax.random.fold_in(stream_key, 6), axis_at), (parts,), jnp.float32, low / len(cuts), largest / len(cuts))
        factor_of = factor_of * jnp.repeat(jnp.exp(steps), dims[axis_at] // parts).reshape((-1,) + (1,) * (len(dims) - 1 - axis_at))
    return factor_of


def centred(rng, shape, scale, bound, cuts=(), held_as=jnp.bfloat16):
    drawn = jax.random.normal(rng, shape, jnp.float32) * scale
    if len(cuts) > 0:
        drawn = levels(rng, shape, cuts, -0.22, 0.18) * drawn
    return jnp.clip(drawn, min=-bound, max=bound).astype(held_as)


def setup_inputs(seed: int = 0) -> dict:
    streams_of = jax.random.split(jax.random.key(seed), 5)
    frames = draw_frames(jax.random.fold_in(streams_of[4], 71), 0)
    residual = centred(streams_of[1], (C, TOTAL), 1.0, 6.0, ((0, 4), (1, 64)), jnp.float32)
    coefficients = centred(streams_of[2], (C, TOTAL), 1.0, 6.0, ((0, 4), (1, 64)), jnp.float32)
    block_index = draw_block_index(jax.random.fold_in(streams_of[4], 71), 0)
    return {"frames": frames, "residual": residual, "coefficients": coefficients, "block_index": block_index}


RIDGE = 0.1
WIDTH_SCALE = 2.0

def kernel_block(rows, block_bf, block_sq):
    row_sq = jnp.sum(rows.astype(jnp.float32) ** 2, axis=1)
    inner = jnp.dot(rows.astype(jnp.float32), block_bf.T.astype(jnp.float32), preferred_element_type=jnp.float32)
    dist = row_sq[:, None] + block_sq[None, :] - 2.0 * inner
    return jnp.exp(-WIDTH_SCALE * dist / D)

def reference(frames, residual, coefficients, block_index):
    frame_rows = frames.T
    residual = residual.T
    coefficients = coefficients.T
    grouped = frame_rows.reshape(N_DP, ROWS_DEV, D)
    for step in range(STEPS):
        chosen = block_index[step]
        block_bf = frame_rows[chosen]
        block_sq = jnp.sum(block_bf.astype(jnp.float32) ** 2, axis=1)
        block_res = residual[chosen]
        gram = kernel_block(block_bf, block_bf, block_sq) + RIDGE * jnp.eye(BLOCK, dtype=jnp.float32)
        factor = jnp.linalg.cholesky(gram)
        delta = jax.scipy.linalg.cho_solve((factor, True), block_res)

        def update(rows):
            kern = kernel_block(rows, block_bf, block_sq)
            return jnp.dot(kern, delta, precision=lax.Precision.HIGHEST)
        change = lax.map(update, grouped).reshape(TOTAL, C)
        residual = residual - change
        residual = residual.at[chosen].add(-RIDGE * delta)
        coefficients = coefficients.at[chosen].add(delta)
    return (residual.T, coefficients.T)
```

```python
import jax
import jax.numpy as jnp
from jax import lax
from jax.sharding import PartitionSpec as P

D = 448
STEPS = 2
BLOCK = 512
RIDGE = 0.1
WIDTH_SCALE = 2.0
AXES = ("dp", "feat")


def permutation(move):
    pairs = []
    for d in range(64):
        for g in range(4):
            y, x, z, h, c = move(d // 16, (d // 4) % 4, d % 4, g // 2, g % 2)
            pairs.append((d * 4 + g, ((y % 4) * 16 + (x % 4) * 4 + z % 4) * 4 + (h % 2) * 2 + c % 2))
    return pairs


def shift(value, axis, by):
    def move(y, x, z, h, c):
        at = dict(y=y, x=x, z=z, h=h, c=c)
        at[axis] += by
        return at["y"], at["x"], at["z"], at["h"], at["c"]

    return lax.ppermute(value, AXES, permutation(move))


def parts3(value):
    high = lax.reduce_precision(value, 8, 7)
    rest = value - high
    mid = lax.reduce_precision(rest, 8, 7)
    return high.astype(jnp.bfloat16), mid.astype(jnp.bfloat16), (rest - mid).astype(jnp.bfloat16)


def rolled(chosen, y, x, z):
    value = chosen.reshape(STEPS, 4, 4, 4, 8)
    for axis, at in ((1, y), (2, x), (3, z)):
        value = lax.dynamic_slice_in_dim(jnp.concatenate([value, value], axis=axis), at, 4, axis=axis)
    return value


def gaussian(row_sq, block_sq, inner):
    dist = row_sq[:, None] + block_sq[None, :] - 2.0 * inner
    return jnp.exp(-WIDTH_SCALE * dist / D)


def on_device(frames, residual, coefficients, block_index):
    rows = frames.shape[1]
    dp = lax.axis_index("dp")
    positions = dp * rows + lax.iota(jnp.int32, rows)
    chosen = rolled(block_index, dp // 16, (dp // 4) % 4, dp % 4).reshape(STEPS, BLOCK)
    flat = chosen.reshape(-1)
    select = (flat[:, None] == positions[None, :]).astype(jnp.bfloat16)
    packed = jnp.concatenate([frames, *parts3(residual), jnp.zeros((33, rows), jnp.bfloat16)], axis=0)
    picked = lax.dot_general(select, packed, (((1,), (1,)), ((), ())), preferred_element_type=jnp.float32)
    held = picked.astype(jnp.bfloat16).reshape(STEPS, 4, 128, 256)
    for axis, inner_rows in (("y", 32), ("x", 8), ("z", 0)):
        total = held[:, 0].astype(jnp.float32)
        for k in (1, 2, 3):
            total = total + shift(held[:, k], axis, k).astype(jnp.float32)
        held = total.astype(jnp.bfloat16)
        if inner_rows:
            held = held.reshape(STEPS, 4, inner_rows, 256)
    far = shift(held[:, :, :112], "h", 1)
    held = jnp.concatenate([held[:, :, :112], far, held[:, :, 112:223]], axis=2)
    for axis in ("z", "x", "y"):
        held = jnp.concatenate([held] + [shift(held, axis, -k) for k in (1, 2, 3)], axis=1)
    block_near = held[:, :, :224]
    block_far = shift(block_near, "c", 1)
    block = jnp.concatenate([block_near, block_far], axis=2)
    res = held[:, :, 224:].astype(jnp.float32)
    block_res = res[:, :, :37] + (res[:, :, 37:74] + res[:, :, 74:111])

    near = jnp.concatenate([frames, shift(frames, "h", 1)], axis=0)
    source = jnp.concatenate([near, shift(near, "c", 1)], axis=0)
    source_sq = jnp.sum(source.astype(jnp.float32) ** 2, axis=0)

    block_all = block.reshape(STEPS * BLOCK, D)
    sq = jnp.sum(block_all.astype(jnp.float32) ** 2, axis=1)
    grams = gaussian(sq, sq, jnp.dot(block_all, block_all.T, preferred_element_type=jnp.float32))
    system = jnp.stack([grams[:BLOCK, :BLOCK], grams[BLOCK:, BLOCK:]]) + RIDGE * jnp.eye(BLOCK, dtype=jnp.float32)
    same = (chosen[1][:, None] == chosen[0][None, :]).astype(jnp.float32)
    cross = grams[BLOCK:, :BLOCK] + RIDGE * same
    factor = jnp.linalg.cholesky(system)
    delta0 = jax.scipy.linalg.cho_solve((factor[0], True), block_res[0])
    res1 = block_res[1] - jnp.dot(cross, delta0, precision=lax.Precision.HIGHEST)
    delta1 = jax.scipy.linalg.cho_solve((factor[1], True), res1)
    delta = jnp.concatenate([delta0, delta1], axis=0)

    inner = lax.dot_general(block_all, source, (((1,), (0,)), ((), ())), preferred_element_type=jnp.float32)
    kernel = gaussian(sq, source_sq, inner)
    change = lax.dot_general(delta, kernel, (((0,), (0,)), ((), ())), precision=lax.Precision.HIGHEST)
    placed = lax.dot_general(
        delta, select.astype(jnp.float32), (((0,), (0,)), ((), ())), precision=lax.Precision.HIGHEST
    )
    return (residual - change - RIDGE * placed, coefficients + placed)


def solution(mesh):
    return jax.shard_map(
        on_device,
        mesh=mesh,
        in_specs=(P("feat", "dp"), P("feat", "dp"), P("feat", "dp"), P()),
        out_specs=(P("feat", "dp"), P("feat", "dp")),
        check_vma=False,
    )
```

```python
import math

import jax
import jax.numpy as jnp
from jax import lax
from jax.experimental import pallas as pl
from jax.experimental.pallas import tpu as pltpu
from jax.sharding import PartitionSpec as P

D = 448
STEPS = 2
BLOCK = 512
RIDGE = 0.1
WIDTH_SCALE = 2.0
AXES = ("dp", "feat")
BF16 = jnp.bfloat16
F32 = jnp.float32
ROWS = 37
PANEL = 16
TILE = 512
SCALE = WIDTH_SCALE / D * math.log2(math.e)


def permutation(move):
    pairs = []
    for d in range(64):
        for g in range(4):
            y, x, z, h, c = move(d // 16, (d // 4) % 4, d % 4, g // 2, g % 2)
            pairs.append((d * 4 + g, ((y % 4) * 16 + (x % 4) * 4 + z % 4) * 4 + (h % 2) * 2 + c % 2))
    return pairs


def shift(value, axis, by):
    def move(y, x, z, h, c):
        at = dict(y=y, x=x, z=z, h=h, c=c)
        at[axis] += by
        return at["y"], at["x"], at["z"], at["h"], at["c"]

    return lax.ppermute(value, AXES, permutation(move))


def parts3(value):
    high = lax.reduce_precision(value, 8, 7)
    rest = value - high
    mid = lax.reduce_precision(rest, 8, 7)
    return high.astype(jnp.bfloat16), mid.astype(jnp.bfloat16), (rest - mid).astype(jnp.bfloat16)


def rolled(chosen, y, x, z):
    value = chosen.reshape(STEPS, 4, 4, 4, 8)
    for axis, at in ((1, y), (2, x), (3, z)):
        value = lax.dynamic_slice_in_dim(jnp.concatenate([value, value], axis=axis), at, 4, axis=axis)
    return value


def split3(value):
    high = value.astype(BF16)
    rest = value - high.astype(F32)
    mid = rest.astype(BF16)
    low = (rest - mid.astype(F32)).astype(BF16)
    return high, mid, low


def dot(a, b):
    return jnp.dot(a, b, preferred_element_type=F32, precision=lax.Precision.HIGHEST)


def invert(mats):
    lane = lax.broadcasted_iota(jnp.int32, (1, PANEL, 128), 2)
    row = lax.broadcasted_iota(jnp.int32, (1, PANEL, 128), 1)
    lane1 = lax.broadcasted_iota(jnp.int32, (1, 128), 1)
    for k in range(4):
        r0 = 128 * k
        block = slice(r0, r0 + 128)
        for p in range(128 // PANEL):
            b = PANEL * p
            rows = slice(r0 + b, r0 + b + PANEL)
            tiles = [mats[:, rows, 128 * q : 128 * q + 128] for q in range(4)]
            old = tiles[k]
            cols = [jnp.broadcast_to(old[:, :, b + j : b + j + 1], (2, PANEL, 128)) for j in range(PANEL)]
            for j in range(PANEL):
                one = jnp.where(row == j, 1.0, 0.0)
                inv = 1.0 / cols[j][:, j : j + 1, :]
                factor = cols[j] - one
                for q in range(j + 1, PANEL):
                    cols[q] = cols[q] - factor * (cols[q][:, j : j + 1, :] * inv)
                tiles[k] = jnp.where(lane == b + j, one, tiles[k])
                for q in range(4):
                    tiles[q] = tiles[q] - factor * (tiles[q][:, j : j + 1, :] * inv)
            new = jnp.concatenate(tiles, axis=2)
            sign = jnp.where(lane1 < b, -1.0, jnp.where(lane1 < b + PANEL, 0.0, 1.0))
            clear = jnp.where((lane1 >= b) & (lane1 < b + PANEL), 0.0, 1.0)
            for s in range(2):
                h, m, l = split3(old[s] * sign)
                nh, nm, nl = split3(new[s])
                lhs = jnp.concatenate([h, h, m, h, l, m], axis=0)
                rhs = jnp.concatenate([nh, nm, nh, nl, nh, nm], axis=0)
                out = lax.dot_general(lhs, rhs, (((0,), (0,)), ((), ())), preferred_element_type=F32)
                for q in range(4):
                    at = slice(128 * q, 128 * q + 128)
                    held = mats[s, block, at]
                    if q == k:
                        held = held * clear
                    mats[s, block, at] = held - out[:, at]
            mats[:, rows, :] = new
        for s in range(2):
            new = mats[s, block, :]
            for i in ((k + 1) % 4, (k + 2) % 4, (k + 3) % 4):
                at_i = slice(128 * i, 128 * i + 128)
                out = dot(mats[s, at_i, block], new)
                for q in range(4):
                    at = slice(128 * q, 128 * q + 128)
                    held = mats[s, at_i, at] if q != k else 0.0
                    mats[s, at_i, at] = held - out[:, at]


def solve_kernel(near, far, point_row, point_col, delta_ref, sq_ref, mats):
    eye = lax.broadcasted_iota(jnp.int32, (BLOCK, BLOCK), 0) == lax.broadcasted_iota(jnp.int32, (BLOCK, BLOCK), 1)

    def inner(a, b):
        total = 0.0
        for ref in (near, far):
            total = total + lax.dot_general(
                ref[a, :, :256], ref[b, :, :256], (((1,), (1,)), ((), ())), preferred_element_type=F32
            )
        return total

    rows, cols = [], []
    for s in range(STEPS):
        products = inner(s, s)
        diagonal = jnp.where(eye, products, 0.0)
        rows.append(jnp.sum(diagonal, axis=0, keepdims=True))
        cols.append(jnp.sum(diagonal, axis=1, keepdims=True))
        sq_ref[BLOCK * s : BLOCK * s + BLOCK] = cols[s]
        kern = jnp.exp2(-SCALE * (cols[s] + rows[s] - 2.0 * products))
        mats[s] = kern + jnp.where(eye, RIDGE, 0.0)
    cross = jnp.exp2(-SCALE * (cols[1] + rows[0] - 2.0 * inner(1, 0)))
    cross = cross + jnp.where(point_col[...] == point_row[...], RIDGE, 0.0)
    invert(mats)

    def block_res(s):
        part = [near[s, :, 256:384].astype(F32)]
        part.append(pltpu.roll(part[0], 128 - 40, 1))
        part.append(pltpu.roll(part[0], 128 - 80, 1))
        return part[0] + (part[1] + part[2])

    delta = dot(mats[0], block_res(0))
    for s in range(STEPS):
        if s == 1:
            delta = dot(mats[1], block_res(1) - dot(cross, delta))
        parts = split3(delta.T[:40])
        pad = jnp.zeros((8, BLOCK), F32)
        stacked = jnp.concatenate([v.astype(F32) for v in parts] + [pad], axis=0)
        delta_ref[:, BLOCK * s : BLOCK * s + BLOCK] = stacked.astype(BF16)


def solve(near, far, chosen):
    return pl.pallas_call(
        solve_kernel,
        out_shape=(
            jax.ShapeDtypeStruct((128, STEPS * BLOCK), BF16),
            jax.ShapeDtypeStruct((STEPS * BLOCK, 1), F32),
        ),
        scratch_shapes=[pltpu.VMEM((2, BLOCK, BLOCK), F32)],
        compiler_params=pltpu.CompilerParams(vmem_limit_bytes=40 << 20),
        name="solve",
    )(near, far, chosen[0].reshape(1, BLOCK), chosen[1].reshape(BLOCK, 1))


def update_kernel(s0, s1, s2, s3, residual, coefficients, near, far, delta, sq, local, res_out, coef_out):
    def squares(ref):
        value = ref[...].astype(F32)
        return jnp.sum(value * value, axis=0, keepdims=True)

    source_sq = squares(s0) + squares(s1) + squares(s2) + squares(s3)
    pad = jnp.zeros((32, TILE), BF16)
    source_near = jnp.concatenate([s0[...], s1[...], pad], axis=0)
    source_far = jnp.concatenate([s2[...], s3[...], pad], axis=0)
    positions = pl.program_id(0) * TILE + lax.broadcasted_iota(jnp.int32, (1, TILE), 1)
    change = jnp.zeros((128, TILE), F32)
    placed = jnp.zeros((128, TILE), F32)
    size = 256
    for c in range(STEPS * BLOCK // size):
        at = slice(size * c, size * c + size)
        s, here = (size * c) // BLOCK, slice((size * c) % BLOCK, (size * c) % BLOCK + size)
        products = jnp.dot(near[s, here, :256], source_near, preferred_element_type=F32)
        products = products + jnp.dot(far[s, here, :256], source_far, preferred_element_type=F32)
        kern = jnp.exp2(-SCALE * (sq[at] + source_sq - 2.0 * products))
        high = kern.astype(BF16)
        low = (kern - high.astype(F32)).astype(BF16)
        here = jnp.where(local[at] == positions, 1.0, 0.0).astype(BF16)
        weights = delta[:, at]
        change = change + jnp.dot(weights, high, preferred_element_type=F32)
        change = change + jnp.dot(weights, low, preferred_element_type=F32)
        placed = placed + jnp.dot(weights, here, preferred_element_type=F32)
    change = change[:40] + (change[40:80] + change[80:120])
    placed = placed[:40] + (placed[40:80] + placed[80:120])
    res_out[...] = residual[...] - change[:ROWS] - RIDGE * placed[:ROWS]
    coef_out[...] = coefficients[...] + placed[:ROWS]


def update(sources, residual, coefficients, near, far, delta, sq, local):
    tile = lambda rows: pl.BlockSpec((rows, TILE), lambda i: (0, i))
    whole = pl.BlockSpec(memory_space=pltpu.VMEM)
    rows = residual.shape[1]
    return pl.pallas_call(
        update_kernel,
        grid=(rows // TILE,),
        in_specs=[tile(112)] * 4 + [tile(ROWS)] * 2 + [whole] * 5,
        out_specs=[tile(ROWS)] * 2,
        out_shape=[jax.ShapeDtypeStruct((ROWS, rows), F32)] * 2,
        compiler_params=pltpu.CompilerParams(vmem_limit_bytes=40 << 20),
        name="update",
    )(*sources, residual, coefficients, near, far, delta, sq, local)


def on_device(frames, residual, coefficients, block_index):
    rows = frames.shape[1]
    dp = lax.axis_index("dp")
    positions = dp * rows + lax.iota(jnp.int32, rows)
    chosen = rolled(block_index, dp // 16, (dp // 4) % 4, dp % 4).reshape(STEPS, BLOCK)
    flat = chosen.reshape(-1)
    select = (flat[:, None] == positions[None, :]).astype(jnp.bfloat16)
    three = jnp.zeros((3, rows), BF16)
    high, mid, low = parts3(residual)
    packed = jnp.concatenate(
        [frames, jnp.zeros((16, rows), BF16), high, three, mid, three, low, three, jnp.zeros((8, rows), BF16)], axis=0
    )
    picked = lax.dot_general(select, packed, (((1,), (1,)), ((), ())), preferred_element_type=F32)
    held = picked.astype(jnp.bfloat16).reshape(STEPS, 4, 128, 256)
    for axis, inner_rows in (("y", 32), ("x", 8), ("z", 0)):
        total = held[:, 0].astype(jnp.float32)
        for k in (1, 2, 3):
            total = total + shift(held[:, k], axis, k).astype(jnp.float32)
        held = total.astype(jnp.bfloat16)
        if inner_rows:
            held = held.reshape(STEPS, 4, inner_rows, 256)
    mine = held[:, :, :112]
    held = jnp.concatenate([mine, shift(mine, "h", 1), jnp.zeros((STEPS, 8, 32), BF16), held[:, :, 128:]], axis=2)
    for axis in ("z", "x", "y"):
        held = jnp.concatenate([held] + [shift(held, axis, -k) for k in (1, 2, 3)], axis=1)
    far = shift(held[:, :, :256], "c", 1)

    across = shift(frames, "h", 1)
    sources = (frames, across, shift(frames, "c", 1), shift(across, "c", 1))
    delta, sq = solve(held, far, chosen)
    local = (flat - dp * rows).reshape(-1, 1)
    return update(sources, residual, coefficients, held, far, delta, sq, local)


def solution(mesh):
    return jax.shard_map(
        on_device,
        mesh=mesh,
        in_specs=(P("feat", "dp"), P("feat", "dp"), P("feat", "dp"), P()),
        out_specs=(P("feat", "dp"), P("feat", "dp")),
        check_vma=False,
    )
```

```python
import math

import jax
import jax.numpy as jnp
from jax import lax
from jax.experimental import pallas as pl
from jax.experimental.pallas import tpu as pltpu
from jax.sharding import PartitionSpec as P

D = 448
STEPS = 2
BLOCK = 512
RIDGE = 0.1
WIDTH_SCALE = 2.0
AXES = ("dp", "feat")
BF16 = jnp.bfloat16
F32 = jnp.float32
ROWS = 37
PANEL = 16
TILE = 512
PICK = 1024
SCALE = WIDTH_SCALE / D * math.log2(math.e)


def permutation(move):
    pairs = []
    for d in range(64):
        for g in range(4):
            y, x, z, h, c = move(d // 16, (d // 4) % 4, d % 4, g // 2, g % 2)
            pairs.append((d * 4 + g, ((y % 4) * 16 + (x % 4) * 4 + z % 4) * 4 + (h % 2) * 2 + c % 2))
    return pairs


def swap(value, dh, dc):
    def move(y, x, z, h, c):
        return y, x, z, h + dh, c + dc

    return lax.ppermute(value, AXES, permutation(move))


PLANE = [[r * 4 + z for r in range(16)] for z in range(4)]
LINE = [[(r * 4 + z) * 4 + h * 2 + c for h in range(2) for z in range(4)] for r in range(16) for c in range(2)]


def split3(value):
    high = value.astype(BF16)
    rest = value - high.astype(F32)
    mid = rest.astype(BF16)
    low = (rest - mid.astype(F32)).astype(BF16)
    return high, mid, low


def dot(a, b):
    return jnp.dot(a, b, preferred_element_type=F32, precision=lax.Precision.HIGHEST)


def invert(mats):
    lane = lax.broadcasted_iota(jnp.int32, (1, PANEL, 128), 2)
    row = lax.broadcasted_iota(jnp.int32, (1, PANEL, 128), 1)
    lane1 = lax.broadcasted_iota(jnp.int32, (1, 128), 1)
    for k in range(4):
        r0 = 128 * k
        block = slice(r0, r0 + 128)
        for p in range(128 // PANEL):
            b = PANEL * p
            rows = slice(r0 + b, r0 + b + PANEL)
            tiles = [mats[:, rows, 128 * q : 128 * q + 128] for q in range(4)]
            old = tiles[k]
            cols = [jnp.broadcast_to(old[:, :, b + j : b + j + 1], (2, PANEL, 128)) for j in range(PANEL)]
            for j in range(PANEL):
                one = jnp.where(row == j, 1.0, 0.0)
                inv = 1.0 / cols[j][:, j : j + 1, :]
                factor = cols[j] - one
                for q in range(j + 1, PANEL):
                    cols[q] = cols[q] - factor * (cols[q][:, j : j + 1, :] * inv)
                tiles[k] = jnp.where(lane == b + j, one, tiles[k])
                for q in range(4):
                    tiles[q] = tiles[q] - factor * (tiles[q][:, j : j + 1, :] * inv)
            new = jnp.concatenate(tiles, axis=2)
            sign = jnp.where(lane1 < b, -1.0, jnp.where(lane1 < b + PANEL, 0.0, 1.0))
            clear = jnp.where((lane1 >= b) & (lane1 < b + PANEL), 0.0, 1.0)
            for s in range(2):
                h, m, l = split3(old[s] * sign)
                nh, nm, nl = split3(new[s])
                lhs = jnp.concatenate([h, h, m, h, l, m], axis=0)
                rhs = jnp.concatenate([nh, nm, nh, nl, nh, nm], axis=0)
                out = lax.dot_general(lhs, rhs, (((0,), (0,)), ((), ())), preferred_element_type=F32)
                for q in range(4):
                    at = slice(128 * q, 128 * q + 128)
                    held = mats[s, block, at]
                    if q == k:
                        held = held * clear
                    mats[s, block, at] = held - out[:, at]
            mats[:, rows, :] = new
        for s in range(2):
            new = mats[s, block, :]
            for i in ((k + 1) % 4, (k + 2) % 4, (k + 3) % 4):
                at_i = slice(128 * i, 128 * i + 128)
                out = dot(mats[s, at_i, block], new)
                for q in range(4):
                    at = slice(128 * q, 128 * q + 128)
                    held = mats[s, at_i, at] if q != k else 0.0
                    mats[s, at_i, at] = held - out[:, at]


def pick_kernel(local, frames, residual, out, total, padded):
    step = pl.program_id(0)
    positions = step * PICK + lax.broadcasted_iota(jnp.int32, (1, PICK), 1)
    select = jnp.where(local[...] == positions, 1.0, 0.0).astype(BF16)
    padded[...] = jnp.zeros_like(padded)
    padded[:ROWS] = residual[...]
    parts = [v.astype(F32) for v in split3(padded[...])] + [jnp.zeros((8, PICK), F32)]
    packed = jnp.concatenate(
        [frames[...], jnp.zeros((16, PICK), BF16), jnp.concatenate(parts, axis=0).astype(BF16)], axis=0
    )
    picked = lax.dot_general(select, packed, (((1,), (1,)), ((), ())), preferred_element_type=F32)

    @pl.when(step == 0)
    def _():
        total[...] = picked

    @pl.when(step > 0)
    def _():
        total[...] += picked

    @pl.when(step == pl.num_programs(0) - 1)
    def _():
        out[...] = total[...].astype(BF16)


def pick(local, frames, residual):
    points = local.shape[0]
    return pl.pallas_call(
        pick_kernel,
        grid=(frames.shape[1] // PICK,),
        in_specs=[
            pl.BlockSpec(memory_space=pltpu.VMEM),
            pl.BlockSpec((112, PICK), lambda i: (0, i)),
            pl.BlockSpec((ROWS, PICK), lambda i: (0, i)),
        ],
        out_specs=pl.BlockSpec((points, 256), lambda i: (0, 0)),
        out_shape=jax.ShapeDtypeStruct((points, 256), BF16),
        scratch_shapes=[pltpu.VMEM((points, 256), F32), pltpu.VMEM((40, PICK), F32)],
        compiler_params=pltpu.CompilerParams(vmem_limit_bytes=40 << 20),
        name="pick",
    )(local, frames, residual)


def add_kernel(held, out):
    total = held[0].astype(F32)
    for i in range(1, 16):
        total = total + held[i].astype(F32)
    total = total.astype(BF16)
    for i in range(8):
        out[i] = total


def add(held):
    return pl.pallas_call(add_kernel, out_shape=jax.ShapeDtypeStruct((8, 64, 256), BF16), name="add")(held)


def mix_kernel(place, held, out):
    def total(at):
        value = held[at].astype(F32)
        for i in range(at + 1, at + 4):
            value = value + held[i].astype(F32)
        return value

    sums = total(0), total(4)
    first = place[0] == 0
    mine = jnp.where(first, sums[0], sums[1])
    other = pltpu.roll(jnp.where(first, sums[1], sums[0])[:, :128], 112, 1)
    lane = lax.broadcasted_iota(jnp.int32, (1, 128), 1)
    near = mine[:, :128] + jnp.where(lane >= 112, other, 0.0)
    tail = jnp.where(lane < 112, other, 0.0)
    value = jnp.concatenate([near, tail, mine[:, 128:]], axis=1).astype(BF16)
    for i in range(16):
        out[i] = value


def mix(place, held):
    return pl.pallas_call(
        mix_kernel,
        in_specs=[pl.BlockSpec(memory_space=pltpu.SMEM), pl.BlockSpec(memory_space=pltpu.VMEM)],
        out_shape=jax.ShapeDtypeStruct((16, 64, 384), BF16),
        name="mix",
    )(place, held)


def solve_kernel(near, far, point_row, point_col, delta_ref, sq_ref, mats):
    eye = lax.broadcasted_iota(jnp.int32, (BLOCK, BLOCK), 0) == lax.broadcasted_iota(jnp.int32, (BLOCK, BLOCK), 1)

    def columns(ref, s, at):
        return ref[:, 32 * s : 32 * s + 32, at].reshape(BLOCK, at.stop - at.start)

    def inner(a, b):
        total = 0.0
        for ref in (near, far):
            total = total + lax.dot_general(
                columns(ref, a, slice(0, 256)),
                columns(ref, b, slice(0, 256)),
                (((1,), (1,)), ((), ())),
                preferred_element_type=F32,
            )
        return total

    rows, cols = [], []
    for s in range(STEPS):
        products = inner(s, s)
        diagonal = jnp.where(eye, products, 0.0)
        rows.append(jnp.sum(diagonal, axis=0, keepdims=True))
        cols.append(jnp.sum(diagonal, axis=1, keepdims=True))
        sq_ref[BLOCK * s : BLOCK * s + BLOCK] = cols[s]
        kern = jnp.exp2(-SCALE * (cols[s] + rows[s] - 2.0 * products))
        mats[s] = kern + jnp.where(eye, RIDGE, 0.0)
    cross = jnp.exp2(-SCALE * (cols[1] + rows[0] - 2.0 * inner(1, 0)))
    cross = cross + jnp.where(point_col[...] == point_row[...], RIDGE, 0.0)
    invert(mats)
    lane = lax.broadcasted_iota(jnp.int32, (1, 128), 1)

    def block_res(s):
        both = []
        for ref in (near, far):
            part = [columns(ref, s, slice(256, 384)).astype(F32)]
            part.append(pltpu.roll(part[0], 128 - 40, 1))
            part.append(pltpu.roll(part[0], 128 - 80, 1))
            both.append(jnp.where(lane < 40, part[0] + (part[1] + part[2]), 0.0))
        return both[0] + pltpu.roll(both[1], 64, 1)

    delta = dot(mats[0], block_res(0))
    for s in range(STEPS):
        if s == 1:
            delta = dot(mats[1], block_res(1) - dot(cross, delta))
        turned = delta.T
        pad = jnp.zeros((8, BLOCK), F32)
        stacked = []
        for at in (0, 64):
            stacked += [v.astype(F32) for v in split3(turned[at : at + 40])] + [pad]
        delta_ref[:, BLOCK * s : BLOCK * s + BLOCK] = jnp.concatenate(stacked, axis=0).astype(BF16)


def solve(near, far, chosen):
    return pl.pallas_call(
        solve_kernel,
        out_shape=(
            jax.ShapeDtypeStruct((256, STEPS * BLOCK), BF16),
            jax.ShapeDtypeStruct((STEPS * BLOCK, 1), F32),
        ),
        scratch_shapes=[pltpu.VMEM((2, BLOCK, BLOCK), F32)],
        compiler_params=pltpu.CompilerParams(vmem_limit_bytes=40 << 20),
        name="solve",
    )(near, far, chosen[0].reshape(1, BLOCK), chosen[1].reshape(BLOCK, 1))


def update_kernel(s0, s1, s2, s3, near, far, delta, sq, local, mine_ref, theirs_ref):
    def squares(ref):
        value = ref[...].astype(F32)
        return jnp.sum(value * value, axis=0, keepdims=True)

    source_sq = squares(s0) + squares(s1) + squares(s2) + squares(s3)
    pad = jnp.zeros((32, TILE), BF16)
    source_near = jnp.concatenate([s0[...], s1[...], pad], axis=0)
    source_far = jnp.concatenate([s2[...], s3[...], pad], axis=0)
    positions = pl.program_id(0) * TILE + lax.broadcasted_iota(jnp.int32, (1, TILE), 1)
    change = jnp.zeros((256, TILE), F32)
    placed = jnp.zeros((256, TILE), F32)
    size = 256
    for c in range(STEPS * BLOCK // size):
        at = slice(size * c, size * c + size)
        s, first = (size * c) // BLOCK, (size * c) % BLOCK // 32
        block = slice(first, first + size // 32), slice(32 * s, 32 * s + 32), slice(0, 256)
        products = jnp.dot(near[block].reshape(size, 256), source_near, preferred_element_type=F32)
        products = products + jnp.dot(far[block].reshape(size, 256), source_far, preferred_element_type=F32)
        kern = jnp.exp2(-SCALE * (sq[at] + source_sq - 2.0 * products))
        here = jnp.where(local[at] == positions, 1.0, 0.0).astype(BF16)
        weights = delta[:, at]
        for part in split3(kern):
            change = change + jnp.dot(weights, part, preferred_element_type=F32)
        placed = placed + jnp.dot(weights, here, preferred_element_type=F32)
    for at, out in ((0, mine_ref), (128, theirs_ref)):
        moved = change[at : at + 40] + (change[at + 40 : at + 80] + change[at + 80 : at + 120])
        added = placed[at : at + 40] + (placed[at + 40 : at + 80] + placed[at + 80 : at + 120])
        out[0] = moved + RIDGE * added
        out[1] = added


def update(sources, near, far, delta, sq, local):
    whole = pl.BlockSpec(memory_space=pltpu.VMEM)
    rows = sources[0].shape[1]
    return pl.pallas_call(
        update_kernel,
        grid=(rows // TILE,),
        in_specs=[pl.BlockSpec((112, TILE), lambda i: (0, i))] * 4 + [whole] * 5,
        out_specs=[pl.BlockSpec((2, 40, TILE), lambda i: (0, 0, i))] * 2,
        out_shape=[jax.ShapeDtypeStruct((2, 40, rows), F32)] * 2,
        compiler_params=pltpu.CompilerParams(vmem_limit_bytes=40 << 20),
        name="update",
    )(*sources, near, far, delta, sq, local)


def finish_kernel(place, residual, coefficients, mine, got, res_out, coef_out):
    own = pl.program_id(0) == place[1]
    value = jnp.where(own, mine[...], got[...])
    res_out[...] = residual[...] - value[0, :ROWS]
    coef_out[...] = coefficients[...] + value[1, :ROWS]


def finish(place, residual, coefficients, mine, got):
    whole = pl.BlockSpec(memory_space=pltpu.VMEM)
    half = pl.BlockSpec((ROWS, residual.shape[1] // 2), lambda i: (0, i))
    return pl.pallas_call(
        finish_kernel,
        grid=(2,),
        in_specs=[pl.BlockSpec(memory_space=pltpu.SMEM), half, half, whole, whole],
        out_specs=[half, half],
        out_shape=[jax.ShapeDtypeStruct(residual.shape, F32)] * 2,
        compiler_params=pltpu.CompilerParams(vmem_limit_bytes=40 << 20),
        name="finish",
    )(place, residual, coefficients, mine, got)


def on_device(frames, residual, coefficients, block_index):
    rows = frames.shape[1]
    dp, feat = lax.axis_index("dp"), lax.axis_index("feat")
    h, c = feat // 2, feat % 2
    place = jnp.stack([h, c]).astype(jnp.int32)
    own_half = lax.dynamic_slice_in_dim(frames, c * (rows // 2), rows // 2, axis=1)
    other_half = lax.dynamic_slice_in_dim(frames, (1 - c) * (rows // 2), rows // 2, axis=1)
    across = swap(own_half, 1, 0)
    beside = swap(other_half, 0, 1)

    points = block_index.reshape(STEPS, 16, 32).transpose(1, 0, 2).reshape(-1, 1)
    held = pick(points - dp * rows, frames, residual).reshape(16, 64, 256)
    held = add(lax.all_to_all(held, "dp", 0, 0, axis_index_groups=PLANE, tiled=True))
    held, across = lax.optimization_barrier((held, across))
    held = lax.all_to_all(held, AXES, 0, 0, axis_index_groups=LINE, tiled=True)
    held, other_half = lax.optimization_barrier((held, other_half))
    diagonal = swap(other_half, 1, 1)
    near = lax.all_to_all(mix(place, held), "dp", 0, 0, axis_index_groups=PLANE, tiled=True)
    far = swap(near, 0, 1)

    delta, sq = solve(near, far, block_index)
    local = block_index.reshape(-1, 1) - dp * rows - c * (rows // 2)
    mine, theirs = update((own_half, across, beside, diagonal), near, far, delta, sq, local)
    return finish(place, residual, coefficients, mine, swap(theirs, 0, 1))


def solution(mesh):
    return jax.shard_map(
        on_device,
        mesh=mesh,
        in_specs=(P("feat", "dp"), P("feat", "dp"), P("feat", "dp"), P()),
        out_specs=(P("feat", "dp"), P("feat", "dp")),
        check_vma=False,
    )
```

```python
import math

import jax
import jax.numpy as jnp
from jax import lax
from jax.experimental import pallas as pl
from jax.experimental.pallas import tpu as pltpu
from jax.sharding import PartitionSpec as P

D = 448
STEPS = 2
BLOCK = 512
RIDGE = 0.1
WIDTH_SCALE = 2.0
AXES = ("dp", "feat")
BF16 = jnp.bfloat16
F32 = jnp.float32
ROWS = 37
PANEL = 16
TILE = 512
PICK = 1024
SCALE = WIDTH_SCALE / D * math.log2(math.e)


def permutation(move):
    pairs = []
    for d in range(64):
        for g in range(4):
            y, x, z, h, c = move(d // 16, (d // 4) % 4, d % 4, g // 2, g % 2)
            pairs.append((d * 4 + g, ((y % 4) * 16 + (x % 4) * 4 + z % 4) * 4 + (h % 2) * 2 + c % 2))
    return pairs


def swap(value, dh, dc):
    def move(y, x, z, h, c):
        return y, x, z, h + dh, c + dc

    return lax.ppermute(value, AXES, permutation(move))


PLANE = [[r * 4 + z for r in range(16)] for z in range(4)]
LINE = [[(r * 4 + z) * 4 + h * 2 + c for h in range(2) for z in range(4)] for r in range(16) for c in range(2)]


def split3(value):
    high = value.astype(BF16)
    rest = value - high.astype(F32)
    mid = rest.astype(BF16)
    low = (rest - mid.astype(F32)).astype(BF16)
    return high, mid, low


def dot(a, b):
    return jnp.dot(a, b, preferred_element_type=F32, precision=lax.Precision.HIGHEST)


def invert(mats):
    lane = lax.broadcasted_iota(jnp.int32, (1, PANEL, 128), 2)
    row = lax.broadcasted_iota(jnp.int32, (1, PANEL, 128), 1)
    lane1 = lax.broadcasted_iota(jnp.int32, (1, 128), 1)
    for k in range(4):
        r0 = 128 * k
        block = slice(r0, r0 + 128)
        for p in range(128 // PANEL):
            b = PANEL * p
            rows = slice(r0 + b, r0 + b + PANEL)
            tiles = [mats[:, rows, 128 * q : 128 * q + 128] for q in range(4)]
            old = tiles[k]
            cols = [jnp.broadcast_to(old[:, :, b + j : b + j + 1], (2, PANEL, 128)) for j in range(PANEL)]
            for j in range(PANEL):
                one = jnp.where(row == j, 1.0, 0.0)
                inv = 1.0 / cols[j][:, j : j + 1, :]
                factor = cols[j] - one
                for q in range(j + 1, PANEL):
                    cols[q] = cols[q] - factor * (cols[q][:, j : j + 1, :] * inv)
                tiles[k] = jnp.where(lane == b + j, one, tiles[k])
                for q in range(4):
                    tiles[q] = tiles[q] - factor * (tiles[q][:, j : j + 1, :] * inv)
            new = jnp.concatenate(tiles, axis=2)
            sign = jnp.where(lane1 < b, -1.0, jnp.where(lane1 < b + PANEL, 0.0, 1.0))
            clear = jnp.where((lane1 >= b) & (lane1 < b + PANEL), 0.0, 1.0)
            for s in range(2):
                h, m, l = split3(old[s] * sign)
                nh, nm, nl = split3(new[s])
                lhs = jnp.concatenate([h, h, m, h, l, m], axis=0)
                rhs = jnp.concatenate([nh, nm, nh, nl, nh, nm], axis=0)
                out = lax.dot_general(lhs, rhs, (((0,), (0,)), ((), ())), preferred_element_type=F32)
                for q in range(4):
                    at = slice(128 * q, 128 * q + 128)
                    held = mats[s, block, at]
                    if q == k:
                        held = held * clear
                    mats[s, block, at] = held - out[:, at]
            mats[:, rows, :] = new
        for s in range(2):
            new = mats[s, block, :]
            for i in ((k + 1) % 4, (k + 2) % 4, (k + 3) % 4):
                at_i = slice(128 * i, 128 * i + 128)
                out = dot(mats[s, at_i, block], new)
                for q in range(4):
                    at = slice(128 * q, 128 * q + 128)
                    held = mats[s, at_i, at] if q != k else 0.0
                    mats[s, at_i, at] = held - out[:, at]


def pick_kernel(local, frames, residual, out, total, padded):
    step = pl.program_id(0)
    positions = step * PICK + lax.broadcasted_iota(jnp.int32, (1, PICK), 1)
    select = jnp.where(local[...] == positions, 1.0, 0.0).astype(BF16)
    padded[...] = jnp.zeros_like(padded)
    padded[:ROWS] = residual[...]
    parts = [v.astype(F32) for v in split3(padded[...])] + [jnp.zeros((8, PICK), F32)]
    packed = jnp.concatenate(
        [frames[...], jnp.zeros((16, PICK), BF16), jnp.concatenate(parts, axis=0).astype(BF16)], axis=0
    )
    picked = lax.dot_general(select, packed, (((1,), (1,)), ((), ())), preferred_element_type=F32)

    @pl.when(step == 0)
    def _():
        total[...] = picked

    @pl.when(step > 0)
    def _():
        total[...] += picked

    @pl.when(step == pl.num_programs(0) - 1)
    def _():
        out[...] = total[...].astype(BF16)


def pick(local, frames, residual):
    points = local.shape[0]
    return pl.pallas_call(
        pick_kernel,
        grid=(frames.shape[1] // PICK,),
        in_specs=[
            pl.BlockSpec(memory_space=pltpu.VMEM),
            pl.BlockSpec((112, PICK), lambda i: (0, i)),
            pl.BlockSpec((ROWS, PICK), lambda i: (0, i)),
        ],
        out_specs=pl.BlockSpec((points, 256), lambda i: (0, 0)),
        out_shape=jax.ShapeDtypeStruct((points, 256), BF16),
        scratch_shapes=[pltpu.VMEM((points, 256), F32), pltpu.VMEM((40, PICK), F32)],
        compiler_params=pltpu.CompilerParams(vmem_limit_bytes=60 << 20),
        name="pick",
    )(local, frames, residual)


def add_kernel(held, out):
    total = held[0].astype(F32)
    for i in range(1, 16):
        total = total + held[i].astype(F32)
    total = total.astype(BF16)
    for i in range(8):
        out[i] = total


def add(held):
    return pl.pallas_call(add_kernel, out_shape=jax.ShapeDtypeStruct((8, 64, 256), BF16), name="add")(held)


def mix_kernel(place, held, out):
    def total(at):
        value = held[at].astype(F32)
        for i in range(at + 1, at + 4):
            value = value + held[i].astype(F32)
        return value

    sums = total(0), total(4)
    first = place[0] == 0
    mine = jnp.where(first, sums[0], sums[1])
    other = pltpu.roll(jnp.where(first, sums[1], sums[0])[:, :128], 112, 1)
    lane = lax.broadcasted_iota(jnp.int32, (1, 128), 1)
    near = mine[:, :128] + jnp.where(lane >= 112, other, 0.0)
    tail = jnp.where(lane < 112, other, 0.0)
    value = jnp.concatenate([near, tail, mine[:, 128:]], axis=1).astype(BF16)
    for i in range(16):
        out[i] = value


def mix(place, held):
    return pl.pallas_call(
        mix_kernel,
        in_specs=[pl.BlockSpec(memory_space=pltpu.SMEM), pl.BlockSpec(memory_space=pltpu.VMEM)],
        out_shape=jax.ShapeDtypeStruct((16, 64, 384), BF16),
        name="mix",
    )(place, held)


def solve_kernel(near, far, point_row, point_col, delta_ref, sq_ref, mats):
    eye = lax.broadcasted_iota(jnp.int32, (BLOCK, BLOCK), 0) == lax.broadcasted_iota(jnp.int32, (BLOCK, BLOCK), 1)

    def columns(ref, s, at):
        return ref[:, 32 * s : 32 * s + 32, at].reshape(BLOCK, at.stop - at.start)

    def inner(a, b):
        total = 0.0
        for ref in (near, far):
            total = total + lax.dot_general(
                columns(ref, a, slice(0, 256)),
                columns(ref, b, slice(0, 256)),
                (((1,), (1,)), ((), ())),
                preferred_element_type=F32,
            )
        return total

    rows, cols = [], []
    for s in range(STEPS):
        products = inner(s, s)
        diagonal = jnp.where(eye, products, 0.0)
        rows.append(jnp.sum(diagonal, axis=0, keepdims=True))
        cols.append(jnp.sum(diagonal, axis=1, keepdims=True))
        sq_ref[BLOCK * s : BLOCK * s + BLOCK] = cols[s]
        kern = jnp.exp2(-SCALE * (cols[s] + rows[s] - 2.0 * products))
        mats[s] = kern + jnp.where(eye, RIDGE, 0.0)
    cross = jnp.exp2(-SCALE * (cols[1] + rows[0] - 2.0 * inner(1, 0)))
    cross = cross + jnp.where(point_col[...] == point_row[...], RIDGE, 0.0)
    invert(mats)
    lane = lax.broadcasted_iota(jnp.int32, (1, 128), 1)

    def block_res(s):
        both = []
        for ref in (near, far):
            part = [columns(ref, s, slice(256, 384)).astype(F32)]
            part.append(pltpu.roll(part[0], 128 - 40, 1))
            part.append(pltpu.roll(part[0], 128 - 80, 1))
            both.append(jnp.where(lane < 40, part[0] + (part[1] + part[2]), 0.0))
        return both[0] + pltpu.roll(both[1], 64, 1)

    delta = dot(mats[0], block_res(0))
    for s in range(STEPS):
        if s == 1:
            delta = dot(mats[1], block_res(1) - dot(cross, delta))
        turned = delta.T
        pad = jnp.zeros((8, BLOCK), F32)
        stacked = []
        for at in (0, 64):
            stacked += [v.astype(F32) for v in split3(turned[at : at + 40])] + [pad]
        delta_ref[:, BLOCK * s : BLOCK * s + BLOCK] = jnp.concatenate(stacked, axis=0).astype(BF16)


def solve(near, far, chosen):
    return pl.pallas_call(
        solve_kernel,
        out_shape=(
            jax.ShapeDtypeStruct((256, STEPS * BLOCK), BF16),
            jax.ShapeDtypeStruct((STEPS * BLOCK, 1), F32),
        ),
        scratch_shapes=[pltpu.VMEM((2, BLOCK, BLOCK), F32)],
        compiler_params=pltpu.CompilerParams(vmem_limit_bytes=40 << 20),
        name="solve",
    )(near, far, chosen[0].reshape(1, BLOCK), chosen[1].reshape(BLOCK, 1))


def update_kernel(s0, s1, s2, s3, near, far, delta, sq, local, mine_ref, theirs_ref):
    def squares(ref):
        value = ref[...].astype(F32)
        return jnp.sum(value * value, axis=0, keepdims=True)

    source_sq = squares(s0) + squares(s1) + squares(s2) + squares(s3)
    pad = jnp.zeros((32, TILE), BF16)
    source_near = jnp.concatenate([s0[...], s1[...], pad], axis=0)
    source_far = jnp.concatenate([s2[...], s3[...], pad], axis=0)
    positions = pl.program_id(0) * TILE + lax.broadcasted_iota(jnp.int32, (1, TILE), 1)
    change = jnp.zeros((256, TILE), F32)
    placed = jnp.zeros((256, TILE), F32)
    size = 256
    for c in range(STEPS * BLOCK // size):
        at = slice(size * c, size * c + size)
        s, first = (size * c) // BLOCK, (size * c) % BLOCK // 32
        block = slice(first, first + size // 32), slice(32 * s, 32 * s + 32), slice(0, 256)
        products = jnp.dot(near[block].reshape(size, 256), source_near, preferred_element_type=F32)
        products = products + jnp.dot(far[block].reshape(size, 256), source_far, preferred_element_type=F32)
        kern = jnp.exp2(-SCALE * (sq[at] + source_sq - 2.0 * products))
        here = jnp.where(local[at] == positions, 1.0, 0.0).astype(BF16)
        weights = delta[:, at]
        for part in split3(kern):
            change = change + jnp.dot(weights, part, preferred_element_type=F32)
        placed = placed + jnp.dot(weights, here, preferred_element_type=F32)
    for at, out in ((0, mine_ref), (128, theirs_ref)):
        moved = change[at : at + 40] + (change[at + 40 : at + 80] + change[at + 80 : at + 120])
        added = placed[at : at + 40] + (placed[at + 40 : at + 80] + placed[at + 80 : at + 120])
        out[0] = moved + RIDGE * added
        out[1] = added


def update(sources, near, far, delta, sq, local):
    whole = pl.BlockSpec(memory_space=pltpu.VMEM)
    rows = sources[0].shape[1]
    return pl.pallas_call(
        update_kernel,
        grid=(rows // TILE,),
        in_specs=[pl.BlockSpec((112, TILE), lambda i: (0, i))] * 4 + [whole] * 5,
        out_specs=[pl.BlockSpec((2, 40, TILE), lambda i: (0, 0, i))] * 2,
        out_shape=[jax.ShapeDtypeStruct((2, 40, rows), F32)] * 2,
        compiler_params=pltpu.CompilerParams(vmem_limit_bytes=40 << 20),
        name="update",
    )(*sources, near, far, delta, sq, local)


def finish_kernel(place, residual, coefficients, mine, got, res_out, coef_out):
    own = pl.program_id(0) == place[1]
    value = jnp.where(own, mine[...], got[...])
    res_out[...] = residual[...] - value[0, :ROWS]
    coef_out[...] = coefficients[...] + value[1, :ROWS]


def finish(place, residual, coefficients, mine, got):
    whole = pl.BlockSpec(memory_space=pltpu.VMEM)
    half = pl.BlockSpec((ROWS, residual.shape[1] // 2), lambda i: (0, i))
    return pl.pallas_call(
        finish_kernel,
        grid=(2,),
        in_specs=[pl.BlockSpec(memory_space=pltpu.SMEM), half, half, whole, whole],
        out_specs=[half, half],
        out_shape=[jax.ShapeDtypeStruct(residual.shape, F32)] * 2,
        compiler_params=pltpu.CompilerParams(vmem_limit_bytes=40 << 20),
        name="finish",
    )(place, residual, coefficients, mine, got)


def on_device(frames, residual, coefficients, block_index):
    rows = frames.shape[1]
    dp, feat = lax.axis_index("dp"), lax.axis_index("feat")
    h, c = feat // 2, feat % 2
    place = jnp.stack([h, c]).astype(jnp.int32)
    own_half = lax.dynamic_slice_in_dim(frames, c * (rows // 2), rows // 2, axis=1)
    other_half = lax.dynamic_slice_in_dim(frames, (1 - c) * (rows // 2), rows // 2, axis=1)
    own_half, other_half, block_index = lax.optimization_barrier((own_half, other_half, block_index))
    across = swap(own_half, 1, 0)
    beside = swap(other_half, 0, 1)

    points = block_index.reshape(STEPS, 16, 32).transpose(1, 0, 2).reshape(-1, 1)
    held = pick(points - dp * rows, frames, residual).reshape(16, 64, 256)
    held = add(lax.all_to_all(held, "dp", 0, 0, axis_index_groups=PLANE, tiled=True))
    held, across = lax.optimization_barrier((held, across))
    held = lax.all_to_all(held, AXES, 0, 0, axis_index_groups=LINE, tiled=True)
    held, other_half = lax.optimization_barrier((held, other_half))
    diagonal = swap(other_half, 1, 1)
    near = lax.all_to_all(mix(place, held), "dp", 0, 0, axis_index_groups=PLANE, tiled=True)
    far = swap(near, 0, 1)

    delta, sq = solve(near, far, block_index)
    local = block_index.reshape(-1, 1) - dp * rows - c * (rows // 2)
    mine, theirs = update((own_half, across, beside, diagonal), near, far, delta, sq, local)
    return finish(place, residual, coefficients, mine, swap(theirs, 0, 1))


def solution(mesh):
    return jax.shard_map(
        on_device,
        mesh=mesh,
        in_specs=(P("feat", "dp"), P("feat", "dp"), P("feat", "dp"), P()),
        out_specs=(P("feat", "dp"), P("feat", "dp")),
        check_vma=False,
    )
```

```python
import math

import jax
import jax.numpy as jnp
from jax import lax
from jax.experimental import pallas as pl
from jax.experimental.pallas import tpu as pltpu
from jax.sharding import PartitionSpec as P

D = 448
STEPS = 2
BLOCK = 512
RIDGE = 0.1
WIDTH_SCALE = 2.0
AXES = ("dp", "feat")
BF16 = jnp.bfloat16
F32 = jnp.float32
ROWS = 37
PANEL = 16
TILE = 512
PICK = 1024
SCALE = WIDTH_SCALE / D * math.log2(math.e)


def permutation(move):
    pairs = []
    for d in range(64):
        for g in range(4):
            y, x, z, h, c = move(d // 16, (d // 4) % 4, d % 4, g // 2, g % 2)
            pairs.append((d * 4 + g, ((y % 4) * 16 + (x % 4) * 4 + z % 4) * 4 + (h % 2) * 2 + c % 2))
    return pairs


def swap(value, dh, dc):
    def move(y, x, z, h, c):
        return y, x, z, h + dh, c + dc

    return lax.ppermute(value, AXES, permutation(move))


PLANE = [[r * 4 + z for r in range(16)] for z in range(4)]
LINE = [[(r * 4 + z) * 4 + h * 2 + c for h in range(2) for z in range(4)] for r in range(16) for c in range(2)]


def split3(value):
    high = value.astype(BF16)
    rest = value - high.astype(F32)
    mid = rest.astype(BF16)
    low = (rest - mid.astype(F32)).astype(BF16)
    return high, mid, low


def dot(a, b):
    ah, am, al = split3(a)
    bh, bm, bl = split3(b)
    lhs = jnp.concatenate([al, ah, am, am, ah, ah], axis=1)
    rhs = jnp.concatenate([bh, bl, bm, bh, bm, bh], axis=0)
    return jnp.dot(lhs, rhs, preferred_element_type=F32)


def dot_rows(a, b):
    ah, am, al = split3(a)
    n = a.shape[0]
    total = 0.0
    for value, lhs in zip(reversed(split3(b)), ((ah,), (am, ah), (al, am, ah))):
        out = jnp.dot(jnp.concatenate(lhs, axis=0), value, preferred_element_type=F32)
        for i in range(len(lhs)):
            total = total + out[n * i : n * i + n]
    return total


def invert(mats, packed):
    lane = lax.broadcasted_iota(jnp.int32, (1, 128), 1)
    lower = lane < 64
    row = lax.broadcasted_iota(jnp.int32, (PANEL, 128), 0)

    def exchange(one, two):
        return jnp.where(lower, one, pltpu.roll(two, 64, 1)), jnp.where(lower, pltpu.roll(one, 64, 1), two)

    for k in range(4):
        r0 = 128 * k
        block = slice(r0, r0 + 128)
        packed[0], packed[1] = exchange(mats[0, block, block], mats[1, block, block])
        for p in range(128 // PANEL):
            b = PANEL * p
            half, first = b // 64, b % 64
            rows = slice(b, b + PANEL)
            new = [packed[0, rows], packed[1, rows]]
            old = exchange(*new)
            cols = []
            for j in range(first, first + PANEL):
                pair = [jnp.broadcast_to(new[half][:, i : i + 1], (PANEL, 128)) for i in (j, 64 + j)]
                cols.append(jnp.where(lower, *pair))
            for j in range(PANEL):
                one = jnp.where(row == j, 1.0, 0.0)
                factor = (cols[j] - one) * (1.0 / cols[j][j : j + 1])
                for q in range(j + 1, PANEL):
                    cols[q] = cols[q] - factor * cols[q][j : j + 1]
                new[half] = jnp.where((lane & 63) == first + j, one, new[half])
                new = [value - factor * value[j : j + 1] for value in new]
            sign = jnp.where(lane < b, -1.0, jnp.where(lane < b + PANEL, 0.0, 1.0))
            nh, nm, nl = split3(jnp.concatenate(new, axis=1))
            rhs = jnp.concatenate([nh, nm, nh, nl, nh, nm], axis=0)
            outs = []
            for value in old:
                h, m, l = split3(value * sign)
                lhs = jnp.concatenate([h, h, m, h, l, m], axis=0)
                outs.append(lax.dot_general(lhs, rhs, (((0,), (0,)), ((), ())), preferred_element_type=F32))
            for i in range(2):
                at = slice(128 * i, 128 * i + 128)
                held = packed[i]
                if i == half:
                    held = jnp.where(((lane & 63) >= first) & ((lane & 63) < first + PANEL), 0.0, held)
                packed[i] = held - jnp.where(lower, outs[0][:, at], outs[1][:, at])
                packed[i, rows] = new[i]
        mats[0, block, block], mats[1, block, block] = exchange(packed[0], packed[1])
        others = [slice(128 * i, 128 * i + 128) for i in ((k + 1) % 4, (k + 2) % 4, (k + 3) % 4)]
        for s in range(2):
            inverse = mats[s, block, block]
            rest = dot(inverse, jnp.concatenate([mats[s, block, at] for at in others], axis=1))
            left = jnp.concatenate([mats[s, at, block] for at in others], axis=0)
            out = dot(left, jnp.concatenate([inverse, rest], axis=1))
            for i, at_i in enumerate(others):
                here = slice(128 * i, 128 * i + 128)
                mats[s, block, at_i] = rest[:, here]
                mats[s, at_i, block] = -out[here, :128]
                for j, at_j in enumerate(others):
                    mats[s, at_i, at_j] = mats[s, at_i, at_j] - out[here, 128 * j + 128 : 128 * j + 256]


def pick_kernel(local, frames, residual, out, total, padded):
    step = pl.program_id(0)
    positions = step * PICK + lax.broadcasted_iota(jnp.int32, (1, PICK), 1)
    select = jnp.where(local[...] == positions, 1.0, 0.0).astype(BF16)
    padded[...] = jnp.zeros_like(padded)
    padded[:ROWS] = residual[...]
    parts = [v.astype(F32) for v in split3(padded[...])] + [jnp.zeros((8, PICK), F32)]
    packed = jnp.concatenate(
        [frames[...], jnp.zeros((16, PICK), BF16), jnp.concatenate(parts, axis=0).astype(BF16)], axis=0
    )
    picked = lax.dot_general(select, packed, (((1,), (1,)), ((), ())), preferred_element_type=F32)

    @pl.when(step == 0)
    def _():
        total[...] = picked

    @pl.when(step > 0)
    def _():
        total[...] += picked

    @pl.when(step == pl.num_programs(0) - 1)
    def _():
        out[...] = total[...].astype(BF16)


def pick(local, frames, residual):
    points = local.shape[0]
    return pl.pallas_call(
        pick_kernel,
        grid=(frames.shape[1] // PICK,),
        in_specs=[
            pl.BlockSpec(memory_space=pltpu.VMEM),
            pl.BlockSpec((112, PICK), lambda i: (0, i)),
            pl.BlockSpec((ROWS, PICK), lambda i: (0, i)),
        ],
        out_specs=pl.BlockSpec((points, 256), lambda i: (0, 0)),
        out_shape=jax.ShapeDtypeStruct((points, 256), BF16),
        scratch_shapes=[pltpu.VMEM((points, 256), F32), pltpu.VMEM((40, PICK), F32)],
        compiler_params=pltpu.CompilerParams(vmem_limit_bytes=60 << 20),
        name="pick",
    )(local, frames, residual)


def add_kernel(held, out):
    total = held[0].astype(F32)
    for i in range(1, 16):
        total = total + held[i].astype(F32)
    total = total.astype(BF16)
    for i in range(8):
        out[i] = total


def add(held):
    return pl.pallas_call(add_kernel, out_shape=jax.ShapeDtypeStruct((8, 64, 256), BF16), name="add")(held)


def mix_kernel(place, held, out):
    def total(at):
        value = held[at].astype(F32)
        for i in range(at + 1, at + 4):
            value = value + held[i].astype(F32)
        return value

    sums = total(0), total(4)
    first = place[0] == 0
    mine = jnp.where(first, sums[0], sums[1])
    other = pltpu.roll(jnp.where(first, sums[1], sums[0])[:, :128], 112, 1)
    lane = lax.broadcasted_iota(jnp.int32, (1, 128), 1)
    near = mine[:, :128] + jnp.where(lane >= 112, other, 0.0)
    tail = jnp.where(lane < 112, other, 0.0)
    value = jnp.concatenate([near, tail, mine[:, 128:]], axis=1).astype(BF16)
    for i in range(16):
        out[i] = value


def mix(place, held):
    return pl.pallas_call(
        mix_kernel,
        in_specs=[pl.BlockSpec(memory_space=pltpu.SMEM), pl.BlockSpec(memory_space=pltpu.VMEM)],
        out_shape=jax.ShapeDtypeStruct((16, 64, 384), BF16),
        name="mix",
    )(place, held)


def solve_kernel(near, far, point_row, point_col, delta_ref, sq_ref, mats, packed, grams):
    eye = lax.broadcasted_iota(jnp.int32, (BLOCK, BLOCK), 0) == lax.broadcasted_iota(jnp.int32, (BLOCK, BLOCK), 1)

    def columns(ref, s, at):
        return ref[:, 32 * s : 32 * s + 32, at].reshape(BLOCK, at.stop - at.start)

    def inner(a, b):
        total = 0.0
        for ref in (near, far):
            total = total + lax.dot_general(
                columns(ref, a, slice(0, 256)),
                columns(ref, b, slice(0, 256)),
                (((1,), (1,)), ((), ())),
                preferred_element_type=F32,
            )
        return total

    rows, cols = [], []
    for s in range(STEPS):
        products = inner(s, s)
        diagonal = jnp.where(eye, products, 0.0)
        rows.append(jnp.sum(diagonal, axis=0, keepdims=True))
        cols.append(jnp.sum(diagonal, axis=1, keepdims=True))
        sq_ref[BLOCK * s : BLOCK * s + BLOCK] = cols[s]
        kern = jnp.exp2(-SCALE * (cols[s] + rows[s] - 2.0 * products))
        mats[s] = grams[s] = kern + jnp.where(eye, RIDGE, 0.0)
    cross = jnp.exp2(-SCALE * (cols[0] + rows[1] - 2.0 * inner(0, 1)))
    cross = cross + jnp.where(point_col[...] == point_row[...], RIDGE, 0.0)
    lane = lax.broadcasted_iota(jnp.int32, (1, 128), 1)

    def block_res(s):
        both = []
        for ref in (near, far):
            part = [columns(ref, s, slice(256, 384)).astype(F32)]
            part.append(pltpu.roll(part[0], 128 - 40, 1))
            part.append(pltpu.roll(part[0], 128 - 80, 1))
            both.append(jnp.where(lane < 40, part[0] + (part[1] + part[2]), 0.0))
        return (both[0] + pltpu.roll(both[1], 64, 1)).T

    res = [block_res(s) for s in range(STEPS)]
    invert(mats, packed)
    for s in range(STEPS):
        if s == 1:
            res[1] = res[1] - dot_rows(delta, cross)
        delta = dot_rows(res[s], mats[s])
        delta = delta + dot_rows(res[s] - dot_rows(delta, grams[s]), mats[s])
        pad = jnp.zeros((8, BLOCK), F32)
        stacked = []
        for at in (0, 64):
            stacked += [v.astype(F32) for v in split3(delta[at : at + 40])] + [pad]
        delta_ref[:, BLOCK * s : BLOCK * s + BLOCK] = jnp.concatenate(stacked, axis=0).astype(BF16)


def solve(near, far, chosen):
    return pl.pallas_call(
        solve_kernel,
        out_shape=(
            jax.ShapeDtypeStruct((256, STEPS * BLOCK), BF16),
            jax.ShapeDtypeStruct((STEPS * BLOCK, 1), F32),
        ),
        scratch_shapes=[
            pltpu.VMEM((2, BLOCK, BLOCK), F32),
            pltpu.VMEM((2, 128, 128), F32),
            pltpu.VMEM((2, BLOCK, BLOCK), F32),
        ],
        compiler_params=pltpu.CompilerParams(vmem_limit_bytes=40 << 20),
        cost_estimate=pl.CostEstimate(flops=1 << 20, bytes_accessed=1 << 20, transcendentals=0),
        name="solve",
    )(near, far, chosen[1].reshape(1, BLOCK), chosen[0].reshape(BLOCK, 1))


def update_kernel(s0, s1, s2, s3, near, far, delta, sq, local, mine_ref, theirs_ref):
    def squares(ref):
        value = ref[...].astype(F32)
        return jnp.sum(value * value, axis=0, keepdims=True)

    source_sq = squares(s0) + squares(s1) + squares(s2) + squares(s3)
    pad = jnp.zeros((32, TILE), BF16)
    source_near = jnp.concatenate([s0[...], s1[...], pad], axis=0)
    source_far = jnp.concatenate([s2[...], s3[...], pad], axis=0)
    positions = pl.program_id(0) * TILE + lax.broadcasted_iota(jnp.int32, (1, TILE), 1)
    change = jnp.zeros((256, TILE), F32)
    placed = jnp.zeros((256, TILE), F32)
    size = 256
    for c in range(STEPS * BLOCK // size):
        at = slice(size * c, size * c + size)
        s, first = (size * c) // BLOCK, (size * c) % BLOCK // 32
        block = slice(first, first + size // 32), slice(32 * s, 32 * s + 32), slice(0, 256)
        products = jnp.dot(near[block].reshape(size, 256), source_near, preferred_element_type=F32)
        products = products + jnp.dot(far[block].reshape(size, 256), source_far, preferred_element_type=F32)
        kern = jnp.exp2(-SCALE * (sq[at] + source_sq - 2.0 * products))
        here = jnp.where(local[at] == positions, 1.0, 0.0).astype(BF16)
        weights = delta[:, at]
        for part in split3(kern):
            change = change + jnp.dot(weights, part, preferred_element_type=F32)
        placed = placed + jnp.dot(weights, here, preferred_element_type=F32)
    for at, out in ((0, mine_ref), (128, theirs_ref)):
        moved = change[at : at + 40] + (change[at + 40 : at + 80] + change[at + 80 : at + 120])
        added = placed[at : at + 40] + (placed[at + 40 : at + 80] + placed[at + 80 : at + 120])
        out[0] = moved + RIDGE * added
        out[1] = added


def update(sources, near, far, delta, sq, local):
    whole = pl.BlockSpec(memory_space=pltpu.VMEM)
    rows = sources[0].shape[1]
    return pl.pallas_call(
        update_kernel,
        grid=(rows // TILE,),
        in_specs=[pl.BlockSpec((112, TILE), lambda i: (0, i))] * 4 + [whole] * 5,
        out_specs=[pl.BlockSpec((2, 40, TILE), lambda i: (0, 0, i))] * 2,
        out_shape=[jax.ShapeDtypeStruct((2, 40, rows), F32)] * 2,
        compiler_params=pltpu.CompilerParams(vmem_limit_bytes=40 << 20),
        name="update",
    )(*sources, near, far, delta, sq, local)


def finish_kernel(place, residual, coefficients, mine, got, res_out, coef_out):
    own = pl.program_id(0) == place[1]
    value = jnp.where(own, mine[...], got[...])
    res_out[...] = residual[...] - value[0, :ROWS]
    coef_out[...] = coefficients[...] + value[1, :ROWS]


def finish(place, residual, coefficients, mine, got):
    whole = pl.BlockSpec(memory_space=pltpu.VMEM)
    half = pl.BlockSpec((ROWS, residual.shape[1] // 2), lambda i: (0, i))
    return pl.pallas_call(
        finish_kernel,
        grid=(2,),
        in_specs=[pl.BlockSpec(memory_space=pltpu.SMEM), half, half, whole, whole],
        out_specs=[half, half],
        out_shape=[jax.ShapeDtypeStruct(residual.shape, F32)] * 2,
        compiler_params=pltpu.CompilerParams(vmem_limit_bytes=40 << 20),
        name="finish",
    )(place, residual, coefficients, mine, got)


def on_device(frames, residual, coefficients, block_index):
    rows = frames.shape[1]
    dp, feat = lax.axis_index("dp"), lax.axis_index("feat")
    h, c = feat // 2, feat % 2
    place = jnp.stack([h, c]).astype(jnp.int32)
    own_half = lax.dynamic_slice_in_dim(frames, c * (rows // 2), rows // 2, axis=1)
    other_half = lax.dynamic_slice_in_dim(frames, (1 - c) * (rows // 2), rows // 2, axis=1)
    beside = swap(other_half, 0, 1)

    points = block_index.reshape(STEPS, 16, 32).transpose(1, 0, 2).reshape(-1, 1)
    held = pick(points - dp * rows, frames, residual).reshape(16, 64, 256)
    held = add(lax.all_to_all(held, "dp", 0, 0, axis_index_groups=PLANE, tiled=True))
    held = lax.all_to_all(held, AXES, 0, 0, axis_index_groups=LINE, tiled=True)
    held, own_half, other_half = lax.optimization_barrier((held, own_half, other_half))
    across, diagonal = swap(own_half, 1, 0), swap(other_half, 1, 1)
    near = lax.all_to_all(mix(place, held), "dp", 0, 0, axis_index_groups=PLANE, tiled=True)
    far = swap(near, 0, 1)

    delta, sq = solve(near, far, block_index)
    local = block_index.reshape(-1, 1) - dp * rows - c * (rows // 2)
    mine, theirs = update((own_half, across, beside, diagonal), near, far, delta, sq, local)
    return finish(place, residual, coefficients, mine, swap(theirs, 0, 1))


def solution(mesh):
    return jax.shard_map(
        on_device,
        mesh=mesh,
        in_specs=(P("feat", "dp"), P("feat", "dp"), P("feat", "dp"), P()),
        out_specs=(P("feat", "dp"), P("feat", "dp")),
        check_vma=False,
    )
```

```python
import math

import jax
import jax.numpy as jnp
from jax import lax
from jax.experimental import pallas as pl
from jax.experimental.pallas import tpu as pltpu
from jax.sharding import PartitionSpec as P

D = 448
STEPS = 2
BLOCK = 512
RIDGE = 0.1
WIDTH_SCALE = 2.0
AXES = ("dp", "feat")
BF16 = jnp.bfloat16
F32 = jnp.float32
ROWS = 37
PANEL = 16
TILE = 1024
PICK = 1024
SCALE = WIDTH_SCALE / D * math.log2(math.e)


def permutation(move):
    pairs = []
    for d in range(64):
        for g in range(4):
            y, x, z, h, c = move(d // 16, (d // 4) % 4, d % 4, g // 2, g % 2)
            pairs.append((d * 4 + g, ((y % 4) * 16 + (x % 4) * 4 + z % 4) * 4 + (h % 2) * 2 + c % 2))
    return pairs


def swap(value, dh, dc):
    def move(y, x, z, h, c):
        return y, x, z, h + dh, c + dc

    return lax.ppermute(value, AXES, permutation(move))


PLANE = [[r * 4 + z for r in range(16)] for z in range(4)]
LINE = [[(r * 4 + z) * 4 + h * 2 + c for h in range(2) for z in range(4)] for r in range(16) for c in range(2)]


def split3(value):
    high = value.astype(BF16)
    rest = value - high.astype(F32)
    mid = rest.astype(BF16)
    low = (rest - mid.astype(F32)).astype(BF16)
    return high, mid, low


def dot(a, b):
    ah, am, al = split3(a)
    bh, bm, bl = split3(b)
    lhs = jnp.concatenate([al, ah, am, am, ah, ah], axis=1)
    rhs = jnp.concatenate([bh, bl, bm, bh, bm, bh], axis=0)
    return jnp.dot(lhs, rhs, preferred_element_type=F32)


def dot_rows(a, b):
    ah, am, al = split3(a)
    n = a.shape[0]
    total = 0.0
    for value, lhs in zip(reversed(split3(b)), ((ah,), (am, ah), (al, am, ah))):
        out = jnp.dot(jnp.concatenate(lhs, axis=0), value, preferred_element_type=F32)
        for i in range(len(lhs)):
            total = total + out[n * i : n * i + n]
    return total


def invert(mats, packed):
    lane = lax.broadcasted_iota(jnp.int32, (1, 128), 1)
    lower = lane < 64
    row = lax.broadcasted_iota(jnp.int32, (PANEL, 128), 0)

    def exchange(one, two):
        return jnp.where(lower, one, pltpu.roll(two, 64, 1)), jnp.where(lower, pltpu.roll(one, 64, 1), two)

    for k in range(4):
        r0 = 128 * k
        block = slice(r0, r0 + 128)
        packed[0], packed[1] = exchange(mats[0, block, block], mats[1, block, block])
        for p in range(128 // PANEL):
            b = PANEL * p
            half, first = b // 64, b % 64
            rows = slice(b, b + PANEL)
            new = [packed[0, rows], packed[1, rows]]
            old = exchange(*new)
            cols = []
            for j in range(first, first + PANEL):
                pair = [jnp.broadcast_to(new[half][:, i : i + 1], (PANEL, 128)) for i in (j, 64 + j)]
                cols.append(jnp.where(lower, *pair))
            for j in range(PANEL):
                one = jnp.where(row == j, 1.0, 0.0)
                factor = (cols[j] - one) * (1.0 / cols[j][j : j + 1])
                for q in range(j + 1, PANEL):
                    cols[q] = cols[q] - factor * cols[q][j : j + 1]
                new[half] = jnp.where((lane & 63) == first + j, one, new[half])
                new = [value - factor * value[j : j + 1] for value in new]
            sign = jnp.where(lane < b, -1.0, jnp.where(lane < b + PANEL, 0.0, 1.0))
            nh, nm, nl = split3(jnp.concatenate(new, axis=1))
            rhs = jnp.concatenate([nh, nm, nh, nl, nh, nm], axis=0)
            outs = []
            for value in old:
                h, m, l = split3(value * sign)
                lhs = jnp.concatenate([h, h, m, h, l, m], axis=0)
                outs.append(lax.dot_general(lhs, rhs, (((0,), (0,)), ((), ())), preferred_element_type=F32))
            for i in range(2):
                at = slice(128 * i, 128 * i + 128)
                held = packed[i]
                if i == half:
                    held = jnp.where(((lane & 63) >= first) & ((lane & 63) < first + PANEL), 0.0, held)
                packed[i] = held - jnp.where(lower, outs[0][:, at], outs[1][:, at])
                packed[i, rows] = new[i]
        mats[0, block, block], mats[1, block, block] = exchange(packed[0], packed[1])
        others = [slice(128 * i, 128 * i + 128) for i in ((k + 1) % 4, (k + 2) % 4, (k + 3) % 4)]
        for s in range(2):
            inverse = mats[s, block, block]
            rest = dot(inverse, jnp.concatenate([mats[s, block, at] for at in others], axis=1))
            left = jnp.concatenate([mats[s, at, block] for at in others], axis=0)
            out = dot(left, jnp.concatenate([inverse, rest], axis=1))
            for i, at_i in enumerate(others):
                here = slice(128 * i, 128 * i + 128)
                mats[s, block, at_i] = rest[:, here]
                mats[s, at_i, block] = -out[here, :128]
                for j, at_j in enumerate(others):
                    mats[s, at_i, at_j] = mats[s, at_i, at_j] - out[here, 128 * j + 128 : 128 * j + 256]


def pick_kernel(local, frames, residual, out, total, padded):
    step = pl.program_id(0)
    positions = step * PICK + lax.broadcasted_iota(jnp.int32, (1, PICK), 1)
    select = jnp.where(local[...] == positions, 1.0, 0.0).astype(BF16)
    padded[...] = jnp.zeros_like(padded)
    padded[:ROWS] = residual[...]
    parts = [v.astype(F32) for v in split3(padded[...])] + [jnp.zeros((8, PICK), F32)]
    packed = jnp.concatenate(
        [frames[...], jnp.zeros((16, PICK), BF16), jnp.concatenate(parts, axis=0).astype(BF16)], axis=0
    )
    picked = lax.dot_general(select, packed, (((1,), (1,)), ((), ())), preferred_element_type=F32)

    @pl.when(step == 0)
    def _():
        total[...] = picked

    @pl.when(step > 0)
    def _():
        total[...] += picked

    @pl.when(step == pl.num_programs(0) - 1)
    def _():
        out[...] = total[...].astype(BF16)


def pick(local, frames, residual):
    points = local.shape[0]
    return pl.pallas_call(
        pick_kernel,
        grid=(frames.shape[1] // PICK,),
        in_specs=[
            pl.BlockSpec(memory_space=pltpu.VMEM),
            pl.BlockSpec((112, PICK), lambda i: (0, i)),
            pl.BlockSpec((ROWS, PICK), lambda i: (0, i)),
        ],
        out_specs=pl.BlockSpec((points, 256), lambda i: (0, 0)),
        out_shape=jax.ShapeDtypeStruct((points, 256), BF16),
        scratch_shapes=[pltpu.VMEM((points, 256), F32), pltpu.VMEM((40, PICK), F32)],
        compiler_params=pltpu.CompilerParams(vmem_limit_bytes=60 << 20),
        name="pick",
    )(local, frames, residual)


def add_kernel(held, out):
    total = held[0].astype(F32)
    for i in range(1, 16):
        total = total + held[i].astype(F32)
    total = total.astype(BF16)
    for i in range(8):
        out[i] = total


def add(held):
    return pl.pallas_call(add_kernel, out_shape=jax.ShapeDtypeStruct((8, 64, 256), BF16), name="add")(held)


def mix_kernel(place, held, out):
    def total(at):
        value = held[at].astype(F32)
        for i in range(at + 1, at + 4):
            value = value + held[i].astype(F32)
        return value

    sums = total(0), total(4)
    first = place[0] == 0
    mine = jnp.where(first, sums[0], sums[1])
    other = pltpu.roll(jnp.where(first, sums[1], sums[0])[:, :128], 112, 1)
    lane = lax.broadcasted_iota(jnp.int32, (1, 128), 1)
    near = mine[:, :128] + jnp.where(lane >= 112, other, 0.0)
    tail = jnp.where(lane < 112, other, 0.0)
    value = jnp.concatenate([near, tail, mine[:, 128:]], axis=1).astype(BF16)
    for i in range(16):
        out[i] = value


def mix(place, held):
    return pl.pallas_call(
        mix_kernel,
        in_specs=[pl.BlockSpec(memory_space=pltpu.SMEM), pl.BlockSpec(memory_space=pltpu.VMEM)],
        out_shape=jax.ShapeDtypeStruct((16, 64, 384), BF16),
        name="mix",
    )(place, held)


def solve_kernel(near, far, point_row, point_col, delta_ref, sq_ref, mats, packed, grams):
    eye = lax.broadcasted_iota(jnp.int32, (BLOCK, BLOCK), 0) == lax.broadcasted_iota(jnp.int32, (BLOCK, BLOCK), 1)

    def columns(ref, s, at):
        return ref[:, 32 * s : 32 * s + 32, at].reshape(BLOCK, at.stop - at.start)

    def inner(a, b):
        total = 0.0
        for ref in (near, far):
            total = total + lax.dot_general(
                columns(ref, a, slice(0, 256)),
                columns(ref, b, slice(0, 256)),
                (((1,), (1,)), ((), ())),
                preferred_element_type=F32,
            )
        return total

    rows, cols = [], []
    for s in range(STEPS):
        products = inner(s, s)
        diagonal = jnp.where(eye, products, 0.0)
        rows.append(jnp.sum(diagonal, axis=0, keepdims=True))
        cols.append(jnp.sum(diagonal, axis=1, keepdims=True))
        sq_ref[BLOCK * s : BLOCK * s + BLOCK] = cols[s]
        kern = jnp.exp2(-SCALE * (cols[s] + rows[s] - 2.0 * products))
        mats[s] = grams[s] = kern + jnp.where(eye, RIDGE, 0.0)
    cross = jnp.exp2(-SCALE * (cols[0] + rows[1] - 2.0 * inner(0, 1)))
    cross = cross + jnp.where(point_col[...] == point_row[...], RIDGE, 0.0)
    lane = lax.broadcasted_iota(jnp.int32, (1, 128), 1)

    def block_res(s):
        both = []
        for ref in (near, far):
            part = [columns(ref, s, slice(256, 384)).astype(F32)]
            part.append(pltpu.roll(part[0], 128 - 40, 1))
            part.append(pltpu.roll(part[0], 128 - 80, 1))
            both.append(jnp.where(lane < 40, part[0] + (part[1] + part[2]), 0.0))
        return (both[0] + pltpu.roll(both[1], 64, 1)).T

    res = [block_res(s) for s in range(STEPS)]
    invert(mats, packed)
    for s in range(STEPS):
        if s == 1:
            res[1] = res[1] - dot_rows(delta, cross)
        delta = dot_rows(res[s], mats[s])
        delta = delta + dot_rows(res[s] - dot_rows(delta, grams[s]), mats[s])
        pad = jnp.zeros((8, BLOCK), F32)
        stacked = []
        for at in (0, 64):
            stacked += [v.astype(F32) for v in split3(delta[at : at + 40])] + [pad]
        delta_ref[:, BLOCK * s : BLOCK * s + BLOCK] = jnp.concatenate(stacked, axis=0).astype(BF16)


def solve(near, far, chosen):
    return pl.pallas_call(
        solve_kernel,
        out_shape=(
            jax.ShapeDtypeStruct((256, STEPS * BLOCK), BF16),
            jax.ShapeDtypeStruct((STEPS * BLOCK, 1), F32),
        ),
        scratch_shapes=[
            pltpu.VMEM((2, BLOCK, BLOCK), F32),
            pltpu.VMEM((2, 128, 128), F32),
            pltpu.VMEM((2, BLOCK, BLOCK), F32),
        ],
        compiler_params=pltpu.CompilerParams(vmem_limit_bytes=40 << 20),
        cost_estimate=pl.CostEstimate(flops=1 << 20, bytes_accessed=1 << 20, transcendentals=0),
        name="solve",
    )(near, far, chosen[1].reshape(1, BLOCK), chosen[0].reshape(BLOCK, 1))


def update_kernel(s0, s1, s2, s3, near, far, delta, sq, local, mine_ref, theirs_ref):
    def squares(ref):
        value = ref[...].astype(F32)
        return jnp.sum(value * value, axis=0, keepdims=True)

    source_sq = SCALE * (squares(s0) + squares(s1) + squares(s2) + squares(s3))
    pad = jnp.zeros((32, TILE), BF16)
    source_near = jnp.concatenate([s0[...], s1[...], pad], axis=0)
    source_far = jnp.concatenate([s2[...], s3[...], pad], axis=0)
    positions = pl.program_id(0) * TILE + lax.broadcasted_iota(jnp.int32, (1, TILE), 1)
    change = jnp.zeros((256, TILE), F32)
    placed = jnp.zeros((256, TILE), F32)
    size = 512
    for c in range(STEPS * BLOCK // size):
        at = slice(size * c, size * c + size)
        s, first = (size * c) // BLOCK, (size * c) % BLOCK // 32
        block = slice(first, first + size // 32), slice(32 * s, 32 * s + 32), slice(0, 256)
        products = jnp.dot(near[block].reshape(size, 256), source_near, preferred_element_type=F32)
        products = products + jnp.dot(far[block].reshape(size, 256), source_far, preferred_element_type=F32)
        kern = jnp.exp2((2.0 * SCALE) * products - (SCALE * sq[at] + source_sq))
        here = jnp.where(local[at] == positions, 1.0, 0.0).astype(BF16)
        weights = delta[:, at]
        for part in split3(kern):
            change = change + jnp.dot(weights, part, preferred_element_type=F32)
        placed = placed + jnp.dot(weights, here, preferred_element_type=F32)
    for at, out in ((0, mine_ref), (128, theirs_ref)):
        moved = change[at : at + 40] + (change[at + 40 : at + 80] + change[at + 80 : at + 120])
        added = placed[at : at + 40] + (placed[at + 40 : at + 80] + placed[at + 80 : at + 120])
        out[0] = moved + RIDGE * added
        out[1] = added


def update(sources, near, far, delta, sq, local):
    whole = pl.BlockSpec(memory_space=pltpu.VMEM)
    rows = sources[0].shape[1]
    return pl.pallas_call(
        update_kernel,
        grid=(rows // TILE,),
        in_specs=[pl.BlockSpec((112, TILE), lambda i: (0, i))] * 4 + [whole] * 5,
        out_specs=[pl.BlockSpec((2, 40, TILE), lambda i: (0, 0, i))] * 2,
        out_shape=[jax.ShapeDtypeStruct((2, 40, rows), F32)] * 2,
        compiler_params=pltpu.CompilerParams(vmem_limit_bytes=40 << 20),
        name="update",
    )(*sources, near, far, delta, sq, local)


def finish_kernel(place, residual, coefficients, mine, got, res_out, coef_out):
    own = pl.program_id(0) == place[1]
    value = jnp.where(own, mine[...], got[...])
    res_out[...] = residual[...] - value[0, :ROWS]
    coef_out[...] = coefficients[...] + value[1, :ROWS]


def finish(place, residual, coefficients, mine, got):
    whole = pl.BlockSpec(memory_space=pltpu.VMEM)
    half = pl.BlockSpec((ROWS, residual.shape[1] // 2), lambda i: (0, i))
    return pl.pallas_call(
        finish_kernel,
        grid=(2,),
        in_specs=[pl.BlockSpec(memory_space=pltpu.SMEM), half, half, whole, whole],
        out_specs=[half, half],
        out_shape=[jax.ShapeDtypeStruct(residual.shape, F32)] * 2,
        compiler_params=pltpu.CompilerParams(vmem_limit_bytes=40 << 20),
        name="finish",
    )(place, residual, coefficients, mine, got)


def on_device(frames, residual, coefficients, block_index):
    rows = frames.shape[1]
    dp, feat = lax.axis_index("dp"), lax.axis_index("feat")
    h, c = feat // 2, feat % 2
    place = jnp.stack([h, c]).astype(jnp.int32)
    own_half = lax.dynamic_slice_in_dim(frames, c * (rows // 2), rows // 2, axis=1)
    other_half = lax.dynamic_slice_in_dim(frames, (1 - c) * (rows // 2), rows // 2, axis=1)
    beside = swap(other_half, 0, 1)

    points = block_index.reshape(STEPS, 16, 32).transpose(1, 0, 2).reshape(-1, 1)
    held = pick(points - dp * rows, frames, residual).reshape(16, 64, 256)
    held = add(lax.all_to_all(held, "dp", 0, 0, axis_index_groups=PLANE, tiled=True))
    held, beside = lax.optimization_barrier((held, beside))
    held = lax.all_to_all(held, AXES, 0, 0, axis_index_groups=LINE, tiled=True)
    held, own_half, other_half = lax.optimization_barrier((held, own_half, other_half))
    across = swap(own_half, 1, 0)
    near = lax.all_to_all(mix(place, held), "dp", 0, 0, axis_index_groups=PLANE, tiled=True)
    near, across, other_half = lax.optimization_barrier((near, across, other_half))
    diagonal = swap(other_half, 1, 1)
    far = swap(near, 0, 1)

    delta, sq = solve(near, far, block_index)
    local = block_index.reshape(-1, 1) - dp * rows - c * (rows // 2)
    mine, theirs = update((own_half, across, beside, diagonal), near, far, delta, sq, local)
    return finish(place, residual, coefficients, mine, swap(theirs, 0, 1))


def solution(mesh):
    return jax.shard_map(
        on_device,
        mesh=mesh,
        in_specs=(P("feat", "dp"), P("feat", "dp"), P("feat", "dp"), P()),
        out_specs=(P("feat", "dp"), P("feat", "dp")),
        check_vma=False,
    )
```

```python
import math

import jax
import jax.numpy as jnp
from jax import lax
from jax.experimental import pallas as pl
from jax.experimental.pallas import tpu as pltpu
from jax.sharding import PartitionSpec as P

D = 448
STEPS = 2
BLOCK = 512
RIDGE = 0.1
WIDTH_SCALE = 2.0
AXES = ("dp", "feat")
BF16 = jnp.bfloat16
F32 = jnp.float32
ROWS = 37
PANEL = 16
TILE = 1024
PICK = 1024
SCALE = WIDTH_SCALE / D * math.log2(math.e)


def permutation(move):
    pairs = []
    for d in range(64):
        for g in range(4):
            y, x, z, h, c = move(d // 16, (d // 4) % 4, d % 4, g // 2, g % 2)
            pairs.append((d * 4 + g, ((y % 4) * 16 + (x % 4) * 4 + z % 4) * 4 + (h % 2) * 2 + c % 2))
    return pairs


def swap(value, dh, dc):
    def move(y, x, z, h, c):
        return y, x, z, h + dh, c + dc

    return lax.ppermute(value, AXES, permutation(move))


PLANE = [[r * 4 + z for r in range(16)] for z in range(4)]
LINE = [[(r * 4 + z) * 4 + h * 2 + c for h in range(2) for z in range(4)] for r in range(16) for c in range(2)]


def split3(value):
    high = value.astype(BF16)
    rest = value - high.astype(F32)
    mid = rest.astype(BF16)
    low = (rest - mid.astype(F32)).astype(BF16)
    return high, mid, low


def dot(a, b):
    ah, am, al = split3(a)
    bh, bm, bl = split3(b)
    lhs = jnp.concatenate([al, ah, am, am, ah, ah], axis=1)
    rhs = jnp.concatenate([bh, bl, bm, bh, bm, bh], axis=0)
    return jnp.dot(lhs, rhs, preferred_element_type=F32)


def dot_rows(a, b):
    ah, am, al = split3(a)
    n = a.shape[0]
    total = 0.0
    for value, lhs in zip(reversed(split3(b)), ((ah,), (am, ah), (al, am, ah))):
        out = jnp.dot(jnp.concatenate(lhs, axis=0), value, preferred_element_type=F32)
        for i in range(len(lhs)):
            total = total + out[n * i : n * i + n]
    return total


def invert(mats, packed):
    lane = lax.broadcasted_iota(jnp.int32, (1, 128), 1)
    lower = lane < 64
    row = lax.broadcasted_iota(jnp.int32, (PANEL, 128), 0)

    def exchange(one, two):
        return jnp.where(lower, one, pltpu.roll(two, 64, 1)), jnp.where(lower, pltpu.roll(one, 64, 1), two)

    def spread(value, first):
        pairs = [[jnp.broadcast_to(value[:, i : i + 1], (PANEL, 128)) for i in (j, 64 + j)] for j in range(first, first + PANEL)]
        return [jnp.where(lower, *pair) for pair in pairs]

    for k in range(4):
        r0 = 128 * k
        block = slice(r0, r0 + 128)
        packed[0], packed[1] = exchange(mats[0, block, block], mats[1, block, block])
        ahead = [packed[0, :PANEL], packed[1, :PANEL]]
        for p in range(128 // PANEL):
            b = PANEL * p
            half, first = b // 64, b % 64
            rows, after = slice(b, b + PANEL), slice(b + PANEL, b + 2 * PANEL)
            inside = ((lane & 63) >= first) & ((lane & 63) < first + PANEL)
            new = ahead
            old = exchange(*new)
            cols = spread(new[half], first)
            if b + PANEL < 128:
                ahead = [packed[0, after], packed[1, after]]
                left = spread(ahead[half], first)
                ahead[half] = jnp.where(inside, 0.0, ahead[half])
            for j in range(PANEL):
                one = jnp.where(row == j, 1.0, 0.0)
                factor = (cols[j] - one) * (1.0 / cols[j][j : j + 1])
                for q in range(j + 1, PANEL):
                    cols[q] = cols[q] - factor * cols[q][j : j + 1]
                new[half] = jnp.where((lane & 63) == first + j, one, new[half])
                new = [value - factor * value[j : j + 1] for value in new]
            if b + PANEL < 128:
                for j in range(PANEL):
                    ahead = [value - left[j] * add[j : j + 1] for value, add in zip(ahead, new)]
            sign = jnp.where(lane < b, -1.0, jnp.where(lane < b + PANEL, 0.0, 1.0))
            nh, nm, nl = split3(jnp.concatenate(new, axis=1))
            rhs = jnp.concatenate([nh, nm, nh, nl, nh, nm], axis=0)
            outs = []
            for value in old:
                h, m, l = split3(value * sign)
                lhs = jnp.concatenate([h, h, m, h, l, m], axis=0)
                outs.append(lax.dot_general(lhs, rhs, (((0,), (0,)), ((), ())), preferred_element_type=F32))
            for i in range(2):
                at = slice(128 * i, 128 * i + 128)
                held = packed[i]
                if i == half:
                    held = jnp.where(inside, 0.0, held)
                packed[i] = held - jnp.where(lower, outs[0][:, at], outs[1][:, at])
                packed[i, rows] = new[i]
                if b + PANEL < 128:
                    packed[i, after] = ahead[i]
        mats[0, block, block], mats[1, block, block] = exchange(packed[0], packed[1])
        others = [slice(128 * i, 128 * i + 128) for i in ((k + 1) % 4, (k + 2) % 4, (k + 3) % 4)]
        for s in range(2):
            inverse = mats[s, block, block]
            rest = dot(inverse, jnp.concatenate([mats[s, block, at] for at in others], axis=1))
            left = jnp.concatenate([mats[s, at, block] for at in others], axis=0)
            out = dot(left, jnp.concatenate([inverse, rest], axis=1))
            for i, at_i in enumerate(others):
                here = slice(128 * i, 128 * i + 128)
                mats[s, block, at_i] = rest[:, here]
                mats[s, at_i, block] = -out[here, :128]
                for j, at_j in enumerate(others):
                    mats[s, at_i, at_j] = mats[s, at_i, at_j] - out[here, 128 * j + 128 : 128 * j + 256]


def pick_kernel(local, frames, residual, out, total, padded):
    step = pl.program_id(0)
    positions = step * PICK + lax.broadcasted_iota(jnp.int32, (1, PICK), 1)
    select = jnp.where(local[...] == positions, 1.0, 0.0).astype(BF16)
    padded[...] = jnp.zeros_like(padded)
    padded[:ROWS] = residual[...]
    parts = [v.astype(F32) for v in split3(padded[...])] + [jnp.zeros((8, PICK), F32)]
    packed = jnp.concatenate(
        [frames[...], jnp.zeros((16, PICK), BF16), jnp.concatenate(parts, axis=0).astype(BF16)], axis=0
    )
    picked = lax.dot_general(select, packed, (((1,), (1,)), ((), ())), preferred_element_type=F32)

    @pl.when(step == 0)
    def _():
        total[...] = picked

    @pl.when(step > 0)
    def _():
        total[...] += picked

    @pl.when(step == pl.num_programs(0) - 1)
    def _():
        out[...] = total[...].astype(BF16)


def pick(local, frames, residual):
    points = local.shape[0]
    return pl.pallas_call(
        pick_kernel,
        grid=(frames.shape[1] // PICK,),
        in_specs=[
            pl.BlockSpec(memory_space=pltpu.VMEM),
            pl.BlockSpec((112, PICK), lambda i: (0, i)),
            pl.BlockSpec((ROWS, PICK), lambda i: (0, i)),
        ],
        out_specs=pl.BlockSpec((points, 256), lambda i: (0, 0)),
        out_shape=jax.ShapeDtypeStruct((points, 256), BF16),
        scratch_shapes=[pltpu.VMEM((points, 256), F32), pltpu.VMEM((40, PICK), F32)],
        compiler_params=pltpu.CompilerParams(vmem_limit_bytes=60 << 20),
        name="pick",
    )(local, frames, residual)


def add_kernel(held, out):
    total = held[0].astype(F32)
    for i in range(1, 16):
        total = total + held[i].astype(F32)
    total = total.astype(BF16)
    for i in range(8):
        out[i] = total


def add(held):
    return pl.pallas_call(add_kernel, out_shape=jax.ShapeDtypeStruct((8, 64, 256), BF16), name="add")(held)


def mix_kernel(place, held, out):
    def total(at):
        value = held[at].astype(F32)
        for i in range(at + 1, at + 4):
            value = value + held[i].astype(F32)
        return value

    sums = total(0), total(4)
    first = place[0] == 0
    mine = jnp.where(first, sums[0], sums[1])
    other = pltpu.roll(jnp.where(first, sums[1], sums[0])[:, :128], 112, 1)
    lane = lax.broadcasted_iota(jnp.int32, (1, 128), 1)
    near = mine[:, :128] + jnp.where(lane >= 112, other, 0.0)
    tail = jnp.where(lane < 112, other, 0.0)
    value = jnp.concatenate([near, tail, mine[:, 128:]], axis=1).astype(BF16)
    for i in range(16):
        out[i] = value


def mix(place, held):
    return pl.pallas_call(
        mix_kernel,
        in_specs=[pl.BlockSpec(memory_space=pltpu.SMEM), pl.BlockSpec(memory_space=pltpu.VMEM)],
        out_shape=jax.ShapeDtypeStruct((16, 64, 384), BF16),
        name="mix",
    )(place, held)


def solve_kernel(near, far, point_row, point_col, delta_ref, sq_ref, mats, packed, grams):
    eye = lax.broadcasted_iota(jnp.int32, (BLOCK, BLOCK), 0) == lax.broadcasted_iota(jnp.int32, (BLOCK, BLOCK), 1)

    def columns(ref, s, at):
        return ref[:, 32 * s : 32 * s + 32, at].reshape(BLOCK, at.stop - at.start)

    def inner(a, b):
        total = 0.0
        for ref in (near, far):
            total = total + lax.dot_general(
                columns(ref, a, slice(0, 256)),
                columns(ref, b, slice(0, 256)),
                (((1,), (1,)), ((), ())),
                preferred_element_type=F32,
            )
        return total

    rows, cols = [], []
    for s in range(STEPS):
        products = inner(s, s)
        diagonal = jnp.where(eye, products, 0.0)
        rows.append(jnp.sum(diagonal, axis=0, keepdims=True))
        cols.append(jnp.sum(diagonal, axis=1, keepdims=True))
        sq_ref[BLOCK * s : BLOCK * s + BLOCK] = cols[s]
        kern = jnp.exp2(-SCALE * (cols[s] + rows[s] - 2.0 * products))
        mats[s] = grams[s] = kern + jnp.where(eye, RIDGE, 0.0)
    cross = jnp.exp2(-SCALE * (cols[0] + rows[1] - 2.0 * inner(0, 1)))
    cross = cross + jnp.where(point_col[...] == point_row[...], RIDGE, 0.0)
    lane = lax.broadcasted_iota(jnp.int32, (1, 128), 1)

    def block_res(s):
        both = []
        for ref in (near, far):
            part = [columns(ref, s, slice(256, 384)).astype(F32)]
            part.append(pltpu.roll(part[0], 128 - 40, 1))
            part.append(pltpu.roll(part[0], 128 - 80, 1))
            both.append(jnp.where(lane < 40, part[0] + (part[1] + part[2]), 0.0))
        return (both[0] + pltpu.roll(both[1], 64, 1)).T

    res = [block_res(s) for s in range(STEPS)]
    invert(mats, packed)
    for s in range(STEPS):
        if s == 1:
            res[1] = res[1] - dot_rows(delta, cross)
        delta = dot_rows(res[s], mats[s])
        delta = delta + dot_rows(res[s] - dot_rows(delta, grams[s]), mats[s])
        pad = jnp.zeros((8, BLOCK), F32)
        stacked = []
        for at in (0, 64):
            stacked += [v.astype(F32) for v in split3(delta[at : at + 40])] + [pad]
        delta_ref[:, BLOCK * s : BLOCK * s + BLOCK] = jnp.concatenate(stacked, axis=0).astype(BF16)


def solve(near, far, chosen):
    return pl.pallas_call(
        solve_kernel,
        out_shape=(
            jax.ShapeDtypeStruct((256, STEPS * BLOCK), BF16),
            jax.ShapeDtypeStruct((STEPS * BLOCK, 1), F32),
        ),
        scratch_shapes=[
            pltpu.VMEM((2, BLOCK, BLOCK), F32),
            pltpu.VMEM((2, 128, 128), F32),
            pltpu.VMEM((2, BLOCK, BLOCK), F32),
        ],
        compiler_params=pltpu.CompilerParams(vmem_limit_bytes=40 << 20),
        cost_estimate=pl.CostEstimate(flops=1 << 20, bytes_accessed=1 << 20, transcendentals=0),
        name="solve",
    )(near, far, chosen[1].reshape(1, BLOCK), chosen[0].reshape(BLOCK, 1))


def update_kernel(s0, s2, s3, a0, a1, near, far, delta, sq, local, mine_ref, theirs_ref):
    s1 = jnp.where(pl.program_id(0) == 0, a0[...], a1[...])

    def squares(ref):
        value = ref[...].astype(F32)
        return jnp.sum(value * value, axis=0, keepdims=True)

    source_sq = SCALE * (squares(s0) + squares(s1) + squares(s2) + squares(s3))
    pad = jnp.zeros((32, TILE), BF16)
    source_near = jnp.concatenate([s0[...], s1, pad], axis=0)
    source_far = jnp.concatenate([s2[...], s3[...], pad], axis=0)
    positions = pl.program_id(0) * TILE + lax.broadcasted_iota(jnp.int32, (1, TILE), 1)
    change = jnp.zeros((256, TILE), F32)
    placed = jnp.zeros((256, TILE), F32)
    size = 512
    for c in range(STEPS * BLOCK // size):
        at = slice(size * c, size * c + size)
        s, first = (size * c) // BLOCK, (size * c) % BLOCK // 32
        block = slice(first, first + size // 32), slice(32 * s, 32 * s + 32), slice(0, 256)
        products = jnp.dot(near[block].reshape(size, 256), source_near, preferred_element_type=F32)
        products = products + jnp.dot(far[block].reshape(size, 256), source_far, preferred_element_type=F32)
        kern = jnp.exp2((2.0 * SCALE) * products - (SCALE * sq[at] + source_sq))
        here = jnp.where(local[at] == positions, 1.0, 0.0).astype(BF16)
        weights = delta[:, at]
        for part in split3(kern):
            change = change + jnp.dot(weights, part, preferred_element_type=F32)
        placed = placed + jnp.dot(weights, here, preferred_element_type=F32)
    for at, out in ((0, mine_ref), (128, theirs_ref)):
        moved = change[at : at + 40] + (change[at + 40 : at + 80] + change[at + 80 : at + 120])
        added = placed[at : at + 40] + (placed[at + 40 : at + 80] + placed[at + 80 : at + 120])
        out[0] = moved + RIDGE * added
        out[1] = added


def update(sources, across, near, far, delta, sq, local):
    whole = pl.BlockSpec(memory_space=pltpu.VMEM)
    rows = sources[0].shape[1]
    return pl.pallas_call(
        update_kernel,
        grid=(rows // TILE,),
        in_specs=[pl.BlockSpec((112, TILE), lambda i: (0, i))] * 3 + [whole] * 7,
        out_specs=[pl.BlockSpec((2, 40, TILE), lambda i: (0, 0, i))] * 2,
        out_shape=[jax.ShapeDtypeStruct((2, 40, rows), F32)] * 2,
        compiler_params=pltpu.CompilerParams(vmem_limit_bytes=40 << 20),
        name="update",
    )(*sources, *across, near, far, delta, sq, local)


def finish_kernel(place, residual, coefficients, mine, got, res_out, coef_out):
    own = pl.program_id(0) == place[1]
    value = jnp.where(own, mine[...], got[...])
    res_out[...] = residual[...] - value[0, :ROWS]
    coef_out[...] = coefficients[...] + value[1, :ROWS]


def finish(place, residual, coefficients, mine, got):
    whole = pl.BlockSpec(memory_space=pltpu.VMEM)
    half = pl.BlockSpec((ROWS, residual.shape[1] // 2), lambda i: (0, i))
    return pl.pallas_call(
        finish_kernel,
        grid=(2,),
        in_specs=[pl.BlockSpec(memory_space=pltpu.SMEM), half, half, whole, whole],
        out_specs=[half, half],
        out_shape=[jax.ShapeDtypeStruct(residual.shape, F32)] * 2,
        compiler_params=pltpu.CompilerParams(vmem_limit_bytes=40 << 20),
        name="finish",
    )(place, residual, coefficients, mine, got)


def on_device(frames, residual, coefficients, block_index):
    rows = frames.shape[1]
    dp, feat = lax.axis_index("dp"), lax.axis_index("feat")
    h, c = feat // 2, feat % 2
    place = jnp.stack([h, c]).astype(jnp.int32)
    own_half = lax.dynamic_slice_in_dim(frames, c * (rows // 2), rows // 2, axis=1)
    other_half = lax.dynamic_slice_in_dim(frames, (1 - c) * (rows // 2), rows // 2, axis=1)
    beside = swap(other_half, 0, 1)
    piece = rows // 4
    across = [swap(own_half[:, :piece], 1, 0)]

    points = block_index.reshape(STEPS, 16, 32).transpose(1, 0, 2).reshape(-1, 1)
    held = pick(points - dp * rows, frames, residual).reshape(16, 64, 256)
    held = add(lax.all_to_all(held, "dp", 0, 0, axis_index_groups=PLANE, tiled=True))
    held, beside, across, own_half, other_half = lax.optimization_barrier((held, beside, across, own_half, other_half))
    held = lax.all_to_all(held, AXES, 0, 0, axis_index_groups=LINE, tiled=True)
    held, own_half, other_half = lax.optimization_barrier((held, own_half, other_half))
    across.append(swap(own_half[:, piece:], 1, 0))
    near = lax.all_to_all(mix(place, held), "dp", 0, 0, axis_index_groups=PLANE, tiled=True)
    near, across, other_half = lax.optimization_barrier((near, across, other_half))
    diagonal = swap(other_half, 1, 1)
    far = swap(near, 0, 1)

    delta, sq = solve(near, far, block_index)
    local = block_index.reshape(-1, 1) - dp * rows - c * (rows // 2)
    mine, theirs = update((own_half, beside, diagonal), across, near, far, delta, sq, local)
    return finish(place, residual, coefficients, mine, swap(theirs, 0, 1))


def solution(mesh):
    return jax.shard_map(
        on_device,
        mesh=mesh,
        in_specs=(P("feat", "dp"), P("feat", "dp"), P("feat", "dp"), P()),
        out_specs=(P("feat", "dp"), P("feat", "dp")),
        check_vma=False,
    )
```

```python
import math

import jax
import jax.numpy as jnp
from jax import lax
from jax.experimental import pallas as pl
from jax.experimental.pallas import tpu as pltpu
from jax.sharding import PartitionSpec as P

D = 448
STEPS = 2
BLOCK = 512
RIDGE = 0.1
WIDTH_SCALE = 2.0
AXES = ("dp", "feat")
BF16 = jnp.bfloat16
F32 = jnp.float32
ROWS = 37
PANEL = 16
TILE = 1024
PICK = 1024
SCALE = WIDTH_SCALE / D * math.log2(math.e)


def permutation(move):
    pairs = []
    for d in range(64):
        for g in range(4):
            y, x, z, h, c = move(d // 16, (d // 4) % 4, d % 4, g // 2, g % 2)
            pairs.append((d * 4 + g, ((y % 4) * 16 + (x % 4) * 4 + z % 4) * 4 + (h % 2) * 2 + c % 2))
    return pairs


def swap(value, dh, dc):
    def move(y, x, z, h, c):
        return y, x, z, h + dh, c + dc

    return lax.ppermute(value, AXES, permutation(move))


PLANE = [[r * 4 + z for r in range(16)] for z in range(4)]
LINE = [[(r * 4 + z) * 4 + h * 2 + c for h in range(2) for z in range(4)] for r in range(16) for c in range(2)]


def split3(value):
    high = value.astype(BF16)
    rest = value - high.astype(F32)
    mid = rest.astype(BF16)
    low = (rest - mid.astype(F32)).astype(BF16)
    return high, mid, low


def dot(a, b):
    ah, am, al = split3(a)
    bh, bm, bl = split3(b)
    lhs = jnp.concatenate([al, ah, am, am, ah, ah], axis=1)
    rhs = jnp.concatenate([bh, bl, bm, bh, bm, bh], axis=0)
    return jnp.dot(lhs, rhs, preferred_element_type=F32)


def dot_rows(a, b):
    ah, am, al = split3(a)
    n = a.shape[0]
    total = 0.0
    for value, lhs in zip(reversed(split3(b)), ((ah,), (am, ah), (al, am, ah))):
        out = jnp.dot(jnp.concatenate(lhs, axis=0), value, preferred_element_type=F32)
        for i in range(len(lhs)):
            total = total + out[n * i : n * i + n]
    return total


def invert(mats, packed):
    lane = lax.broadcasted_iota(jnp.int32, (1, 128), 1)
    lower = lane < 64
    row = lax.broadcasted_iota(jnp.int32, (PANEL, 128), 0)

    def exchange(one, two):
        return jnp.where(lower, one, pltpu.roll(two, 64, 1)), jnp.where(lower, pltpu.roll(one, 64, 1), two)

    def spread(value, first):
        pairs = [[jnp.broadcast_to(value[:, i : i + 1], (PANEL, 128)) for i in (j, 64 + j)] for j in range(first, first + PANEL)]
        return [jnp.where(lower, *pair) for pair in pairs]

    for k in range(4):
        r0 = 128 * k
        block = slice(r0, r0 + 128)
        packed[0], packed[1] = exchange(mats[0, block, block], mats[1, block, block])
        ahead = [packed[0, :PANEL], packed[1, :PANEL]]
        for p in range(128 // PANEL):
            b = PANEL * p
            half, first = b // 64, b % 64
            rows, after = slice(b, b + PANEL), slice(b + PANEL, b + 2 * PANEL)
            inside = ((lane & 63) >= first) & ((lane & 63) < first + PANEL)
            new = ahead
            old = exchange(*new)
            cols = spread(new[half], first)
            if b + PANEL < 128:
                ahead = [packed[0, after], packed[1, after]]
                left = spread(ahead[half], first)
                ahead[half] = jnp.where(inside, 0.0, ahead[half])
            for j in range(PANEL):
                one = jnp.where(row == j, 1.0, 0.0)
                factor = (cols[j] - one) * (1.0 / cols[j][j : j + 1])
                for q in range(j + 1, PANEL):
                    cols[q] = cols[q] - factor * cols[q][j : j + 1]
                new[half] = jnp.where((lane & 63) == first + j, one, new[half])
                new = [value - factor * value[j : j + 1] for value in new]
            if b + PANEL < 128:
                for j in range(PANEL):
                    ahead = [value - left[j] * add[j : j + 1] for value, add in zip(ahead, new)]
            sign = jnp.where(lane < b, -1.0, jnp.where(lane < b + PANEL, 0.0, 1.0))
            nh, nm, nl = split3(jnp.concatenate(new, axis=1))
            rhs = jnp.concatenate([nh, nm, nh, nl, nh, nm], axis=0)
            outs = []
            for value in old:
                h, m, l = split3(value * sign)
                lhs = jnp.concatenate([h, h, m, h, l, m], axis=0)
                outs.append(lax.dot_general(lhs, rhs, (((0,), (0,)), ((), ())), preferred_element_type=F32))
            for i in range(2):
                at = slice(128 * i, 128 * i + 128)
                held = packed[i]
                if i == half:
                    held = jnp.where(inside, 0.0, held)
                packed[i] = held - jnp.where(lower, outs[0][:, at], outs[1][:, at])
                packed[i, rows] = new[i]
                if b + PANEL < 128:
                    packed[i, after] = ahead[i]
        mats[0, block, block], mats[1, block, block] = exchange(packed[0], packed[1])
        others = [slice(128 * i, 128 * i + 128) for i in ((k + 1) % 4, (k + 2) % 4, (k + 3) % 4)]
        for s in range(2):
            inverse = mats[s, block, block]
            rest = dot(inverse, jnp.concatenate([mats[s, block, at] for at in others], axis=1))
            left = jnp.concatenate([mats[s, at, block] for at in others], axis=0)
            out = dot(left, jnp.concatenate([inverse, rest], axis=1))
            for i, at_i in enumerate(others):
                here = slice(128 * i, 128 * i + 128)
                mats[s, block, at_i] = rest[:, here]
                mats[s, at_i, block] = -out[here, :128]
                for j, at_j in enumerate(others):
                    mats[s, at_i, at_j] = mats[s, at_i, at_j] - out[here, 128 * j + 128 : 128 * j + 256]


def pick_kernel(place, index, frames, residual, out, total, padded):
    step = pl.program_id(0)
    positions = place[2] + step * PICK + lax.broadcasted_iota(jnp.int32, (PICK, BLOCK), 0)
    padded[...] = jnp.zeros_like(padded)
    padded[:ROWS] = residual[...]
    parts = [v.astype(F32) for v in split3(padded[...])] + [jnp.zeros((8, PICK), F32)]
    packed = jnp.concatenate(
        [frames[...], jnp.zeros((16, PICK), BF16), jnp.concatenate(parts, axis=0).astype(BF16)], axis=0
    )
    picked = []
    for s in range(STEPS):
        select = jnp.where(index[s : s + 1] == positions, 1.0, 0.0).astype(BF16)
        picked.append(jnp.dot(packed, select, preferred_element_type=F32))

    @pl.when(step == 0)
    def _():
        for s in range(STEPS):
            total[s] = picked[s]

    @pl.when(step > 0)
    def _():
        for s in range(STEPS):
            total[s] += picked[s]

    @pl.when(step == pl.num_programs(0) - 1)
    def _():
        for s in range(STEPS):
            out[:, 32 * s : 32 * s + 32] = total[s].T.astype(BF16).reshape(16, 32, 256)


def pick(place, index, frames, residual):
    return pl.pallas_call(
        pick_kernel,
        grid=(frames.shape[1] // PICK,),
        in_specs=[
            pl.BlockSpec(memory_space=pltpu.SMEM),
            pl.BlockSpec(memory_space=pltpu.VMEM),
            pl.BlockSpec((112, PICK), lambda i: (0, i)),
            pl.BlockSpec((ROWS, PICK), lambda i: (0, i)),
        ],
        out_specs=pl.BlockSpec((16, 64, 256), lambda i: (0, 0, 0)),
        out_shape=jax.ShapeDtypeStruct((16, 64, 256), BF16),
        scratch_shapes=[pltpu.VMEM((STEPS, 256, BLOCK), F32), pltpu.VMEM((40, PICK), F32)],
        compiler_params=pltpu.CompilerParams(vmem_limit_bytes=60 << 20),
        name="pick",
    )(place, index, frames, residual)


def add_kernel(held, out):
    total = held[0].astype(F32)
    for i in range(1, 16):
        total = total + held[i].astype(F32)
    total = total.astype(BF16)
    for i in range(8):
        out[i] = total


def add(held):
    return pl.pallas_call(add_kernel, out_shape=jax.ShapeDtypeStruct((8, 64, 256), BF16), name="add")(held)


def mix_kernel(place, held, out):
    def total(at):
        value = held[at].astype(F32)
        for i in range(at + 1, at + 4):
            value = value + held[i].astype(F32)
        return value

    sums = total(0), total(4)
    first = place[0] == 0
    mine = jnp.where(first, sums[0], sums[1])
    other = pltpu.roll(jnp.where(first, sums[1], sums[0])[:, :128], 112, 1)
    lane = lax.broadcasted_iota(jnp.int32, (1, 128), 1)
    near = mine[:, :128] + jnp.where(lane >= 112, other, 0.0)
    tail = jnp.where(lane < 112, other, 0.0)
    value = jnp.concatenate([near, tail, mine[:, 128:]], axis=1).astype(BF16)
    for i in range(16):
        out[i] = value


def mix(place, held):
    return pl.pallas_call(
        mix_kernel,
        in_specs=[pl.BlockSpec(memory_space=pltpu.SMEM), pl.BlockSpec(memory_space=pltpu.VMEM)],
        out_shape=jax.ShapeDtypeStruct((16, 64, 384), BF16),
        name="mix",
    )(place, held)


def solve_kernel(near, far, point_row, point_col, delta_ref, sq_ref, mats, packed, grams):
    eye = lax.broadcasted_iota(jnp.int32, (BLOCK, BLOCK), 0) == lax.broadcasted_iota(jnp.int32, (BLOCK, BLOCK), 1)

    def columns(ref, s, at):
        return ref[:, 32 * s : 32 * s + 32, at].reshape(BLOCK, at.stop - at.start)

    def inner(a, b):
        total = 0.0
        for ref in (near, far):
            total = total + lax.dot_general(
                columns(ref, a, slice(0, 256)),
                columns(ref, b, slice(0, 256)),
                (((1,), (1,)), ((), ())),
                preferred_element_type=F32,
            )
        return total

    rows, cols = [], []
    for s in range(STEPS):
        products = inner(s, s)
        diagonal = jnp.where(eye, products, 0.0)
        rows.append(jnp.sum(diagonal, axis=0, keepdims=True))
        cols.append(jnp.sum(diagonal, axis=1, keepdims=True))
        sq_ref[BLOCK * s : BLOCK * s + BLOCK] = cols[s]
        kern = jnp.exp2(-SCALE * (cols[s] + rows[s] - 2.0 * products))
        mats[s] = grams[s] = kern + jnp.where(eye, RIDGE, 0.0)
    cross = jnp.exp2(-SCALE * (cols[0] + rows[1] - 2.0 * inner(0, 1)))
    cross = cross + jnp.where(point_col[...] == point_row[...], RIDGE, 0.0)
    lane = lax.broadcasted_iota(jnp.int32, (1, 128), 1)

    def block_res(s):
        both = []
        for ref in (near, far):
            part = [columns(ref, s, slice(256, 384)).astype(F32)]
            part.append(pltpu.roll(part[0], 128 - 40, 1))
            part.append(pltpu.roll(part[0], 128 - 80, 1))
            both.append(jnp.where(lane < 40, part[0] + (part[1] + part[2]), 0.0))
        return (both[0] + pltpu.roll(both[1], 64, 1)).T

    res = [block_res(s) for s in range(STEPS)]
    invert(mats, packed)
    for s in range(STEPS):
        if s == 1:
            res[1] = res[1] - dot_rows(delta, cross)
        delta = dot_rows(res[s], mats[s])
        delta = delta + dot_rows(res[s] - dot_rows(delta, grams[s]), mats[s])
        pad = jnp.zeros((8, BLOCK), F32)
        stacked = []
        for at in (0, 64):
            stacked += [v.astype(F32) for v in split3(delta[at : at + 40])] + [pad]
        delta_ref[:, BLOCK * s : BLOCK * s + BLOCK] = jnp.concatenate(stacked, axis=0).astype(BF16)


def solve(near, far, chosen):
    return pl.pallas_call(
        solve_kernel,
        out_shape=(
            jax.ShapeDtypeStruct((256, STEPS * BLOCK), BF16),
            jax.ShapeDtypeStruct((STEPS * BLOCK, 1), F32),
        ),
        scratch_shapes=[
            pltpu.VMEM((2, BLOCK, BLOCK), F32),
            pltpu.VMEM((2, 128, 128), F32),
            pltpu.VMEM((2, BLOCK, BLOCK), F32),
        ],
        compiler_params=pltpu.CompilerParams(vmem_limit_bytes=40 << 20),
        cost_estimate=pl.CostEstimate(flops=1 << 20, bytes_accessed=1 << 20, transcendentals=0),
        name="solve",
    )(near, far, chosen[1].reshape(1, BLOCK), chosen[0].reshape(BLOCK, 1))


def update_kernel(s0, s2, s3, a0, a1, a2, a3, near, far, delta, sq, local, mine_ref, theirs_ref):
    pieces = [jnp.concatenate([one[...], two[...]], axis=1) for one, two in ((a0, a1), (a2, a3))]
    s1 = jnp.where(pl.program_id(0) == 0, *pieces)

    def squares(ref):
        value = ref[...].astype(F32)
        return jnp.sum(value * value, axis=0, keepdims=True)

    source_sq = SCALE * (squares(s0) + squares(s1) + squares(s2) + squares(s3))
    pad = jnp.zeros((32, TILE), BF16)
    source_near = jnp.concatenate([s0[...], s1, pad], axis=0)
    source_far = jnp.concatenate([s2[...], s3[...], pad], axis=0)
    positions = pl.program_id(0) * TILE + lax.broadcasted_iota(jnp.int32, (1, TILE), 1)
    change = jnp.zeros((256, TILE), F32)
    placed = jnp.zeros((256, TILE), F32)
    size = 512
    for c in range(STEPS * BLOCK // size):
        at = slice(size * c, size * c + size)
        s, first = (size * c) // BLOCK, (size * c) % BLOCK // 32
        block = slice(first, first + size // 32), slice(32 * s, 32 * s + 32), slice(0, 256)
        products = jnp.dot(near[block].reshape(size, 256), source_near, preferred_element_type=F32)
        products = products + jnp.dot(far[block].reshape(size, 256), source_far, preferred_element_type=F32)
        kern = jnp.exp2((2.0 * SCALE) * products - (SCALE * sq[at] + source_sq))
        here = jnp.where(local[at] == positions, 1.0, 0.0).astype(BF16)
        weights = delta[:, at]
        for part in split3(kern):
            change = change + jnp.dot(weights, part, preferred_element_type=F32)
        placed = placed + jnp.dot(weights, here, preferred_element_type=F32)
    for at, out in ((0, mine_ref), (128, theirs_ref)):
        moved = change[at : at + 40] + (change[at + 40 : at + 80] + change[at + 80 : at + 120])
        added = placed[at : at + 40] + (placed[at + 40 : at + 80] + placed[at + 80 : at + 120])
        out[0] = moved + RIDGE * added
        out[1] = added


def update(sources, across, near, far, delta, sq, local):
    whole = pl.BlockSpec(memory_space=pltpu.VMEM)
    rows = sources[0].shape[1]
    return pl.pallas_call(
        update_kernel,
        grid=(rows // TILE,),
        in_specs=[pl.BlockSpec((112, TILE), lambda i: (0, i))] * 3 + [whole] * 9,
        out_specs=[pl.BlockSpec((2, 40, TILE), lambda i: (0, 0, i))] * 2,
        out_shape=[jax.ShapeDtypeStruct((2, 40, rows), F32)] * 2,
        compiler_params=pltpu.CompilerParams(vmem_limit_bytes=40 << 20),
        name="update",
    )(*sources, *across, near, far, delta, sq, local)


def finish_kernel(place, residual, coefficients, mine, got, res_out, coef_out):
    own = pl.program_id(0) == place[1]
    value = jnp.where(own, mine[...], got[...])
    res_out[...] = residual[...] - value[0, :ROWS]
    coef_out[...] = coefficients[...] + value[1, :ROWS]


def finish(place, residual, coefficients, mine, got):
    whole = pl.BlockSpec(memory_space=pltpu.VMEM)
    half = pl.BlockSpec((ROWS, residual.shape[1] // 2), lambda i: (0, i))
    return pl.pallas_call(
        finish_kernel,
        grid=(2,),
        in_specs=[pl.BlockSpec(memory_space=pltpu.SMEM), half, half, whole, whole],
        out_specs=[half, half],
        out_shape=[jax.ShapeDtypeStruct(residual.shape, F32)] * 2,
        compiler_params=pltpu.CompilerParams(vmem_limit_bytes=40 << 20),
        name="finish",
    )(place, residual, coefficients, mine, got)


def on_device(frames, residual, coefficients, block_index):
    rows = frames.shape[1]
    dp, feat = lax.axis_index("dp"), lax.axis_index("feat")
    h, c = feat // 2, feat % 2
    place = jnp.stack([h, c, dp * rows]).astype(jnp.int32)
    own_half = lax.dynamic_slice_in_dim(frames, c * (rows // 2), rows // 2, axis=1)
    other_half = lax.dynamic_slice_in_dim(frames, (1 - c) * (rows // 2), rows // 2, axis=1)
    beside = swap(other_half, 0, 1)
    size = rows // 8
    own = [lax.dynamic_slice_in_dim(frames, c * (rows // 2) + i * size, size, axis=1) for i in range(4)]
    across = [swap(own[0], 1, 0)]

    held = pick(place, block_index, frames, residual)
    held, across, own = lax.optimization_barrier((held, across, own))
    across.append(swap(own[1], 1, 0))
    held = add(lax.all_to_all(held, "dp", 0, 0, axis_index_groups=PLANE, tiled=True))
    held, beside, across, own, other_half = lax.optimization_barrier((held, beside, across, own, other_half))
    held = lax.all_to_all(held, AXES, 0, 0, axis_index_groups=LINE, tiled=True)
    held, own, other_half = lax.optimization_barrier((held, own, other_half))
    across.append(swap(own[2], 1, 0))
    near = lax.all_to_all(mix(place, held), "dp", 0, 0, axis_index_groups=PLANE, tiled=True)
    near, across, own, other_half = lax.optimization_barrier((near, across, own, other_half))
    far = swap(near, 0, 1)
    across.append(swap(own[3], 1, 0))
    diagonal = swap(other_half, 1, 1)

    delta, sq = solve(near, far, block_index)
    local = block_index.reshape(-1, 1) - dp * rows - c * (rows // 2)
    mine, theirs = update((own_half, beside, diagonal), across, near, far, delta, sq, local)
    return finish(place, residual, coefficients, mine, swap(theirs, 0, 1))


def solution(mesh):
    return jax.shard_map(
        on_device,
        mesh=mesh,
        in_specs=(P("feat", "dp"), P("feat", "dp"), P("feat", "dp"), P()),
        out_specs=(P("feat", "dp"), P("feat", "dp")),
        check_vma=False,
    )
```

```python
import math

import jax
import jax.numpy as jnp
from jax import lax
from jax.experimental import pallas as pl
from jax.experimental.pallas import tpu as pltpu
from jax.sharding import PartitionSpec as P

D = 448
STEPS = 2
BLOCK = 512
RIDGE = 0.1
WIDTH_SCALE = 2.0
AXES = ("dp", "feat")
BF16 = jnp.bfloat16
F32 = jnp.float32
ROWS = 37
PANEL = 16
TILE = 1024
PICK = 1024
SCALE = WIDTH_SCALE / D * math.log2(math.e)


def permutation(move):
    pairs = []
    for d in range(64):
        for g in range(4):
            y, x, z, h, c = move(d // 16, (d // 4) % 4, d % 4, g // 2, g % 2)
            pairs.append((d * 4 + g, ((y % 4) * 16 + (x % 4) * 4 + z % 4) * 4 + (h % 2) * 2 + c % 2))
    return pairs


def swap(value, dh, dc):
    def move(y, x, z, h, c):
        return y, x, z, h + dh, c + dc

    return lax.ppermute(value, AXES, permutation(move))


PLANE = [[r * 4 + z for r in range(16)] for z in range(4)]
LINE = [[(r * 4 + z) * 4 + h * 2 + c for h in range(2) for z in range(4)] for r in range(16) for c in range(2)]


def split3(value):
    high = value.astype(BF16)
    rest = value - high.astype(F32)
    mid = rest.astype(BF16)
    low = (rest - mid.astype(F32)).astype(BF16)
    return high, mid, low


def dot(a, b):
    ah, am, al = split3(a)
    bh, bm, bl = split3(b)
    lhs = jnp.concatenate([al, ah, am, am, ah, ah], axis=1)
    rhs = jnp.concatenate([bh, bl, bm, bh, bm, bh], axis=0)
    return jnp.dot(lhs, rhs, preferred_element_type=F32)


def dot_rows(a, b):
    ah, am, al = split3(a)
    n = a.shape[0]
    total = 0.0
    for value, lhs in zip(reversed(split3(b)), ((ah,), (am, ah), (al, am, ah))):
        out = jnp.dot(jnp.concatenate(lhs, axis=0), value, preferred_element_type=F32)
        for i in range(len(lhs)):
            total = total + out[n * i : n * i + n]
    return total


def invert(mats, packed):
    lane = lax.broadcasted_iota(jnp.int32, (1, 128), 1)
    lower = lane < 64
    row = lax.broadcasted_iota(jnp.int32, (PANEL, 128), 0)

    def exchange(one, two):
        return jnp.where(lower, one, pltpu.roll(two, 64, 1)), jnp.where(lower, pltpu.roll(one, 64, 1), two)

    def spread(value, first):
        pairs = [[jnp.broadcast_to(value[:, i : i + 1], (PANEL, 128)) for i in (j, 64 + j)] for j in range(first, first + PANEL)]
        return [jnp.where(lower, *pair) for pair in pairs]

    for k in range(4):
        r0 = 128 * k
        block = slice(r0, r0 + 128)
        packed[0], packed[1] = exchange(mats[0, block, block], mats[1, block, block])
        ahead = [packed[0, :PANEL], packed[1, :PANEL]]
        for p in range(128 // PANEL):
            b = PANEL * p
            half, first = b // 64, b % 64
            rows, after = slice(b, b + PANEL), slice(b + PANEL, b + 2 * PANEL)
            inside = ((lane & 63) >= first) & ((lane & 63) < first + PANEL)
            new = ahead
            old = exchange(*new)
            cols = spread(new[half], first)
            if b + PANEL < 128:
                ahead = [packed[0, after], packed[1, after]]
                left = spread(ahead[half], first)
                ahead[half] = jnp.where(inside, 0.0, ahead[half])
            for j in range(PANEL):
                one = jnp.where(row == j, 1.0, 0.0)
                factor = (cols[j] - one) * (1.0 / cols[j][j : j + 1])
                for q in range(j + 1, PANEL):
                    cols[q] = cols[q] - factor * cols[q][j : j + 1]
                new[half] = jnp.where((lane & 63) == first + j, one, new[half])
                new = [value - factor * value[j : j + 1] for value in new]
            if b + PANEL < 128:
                for j in range(PANEL):
                    ahead = [value - left[j] * add[j : j + 1] for value, add in zip(ahead, new)]
            sign = jnp.where(lane < b, -1.0, jnp.where(lane < b + PANEL, 0.0, 1.0))
            nh, nm, nl = split3(jnp.concatenate(new, axis=1))
            rhs = jnp.concatenate([nh, nm, nh, nl, nh, nm], axis=0)
            outs = []
            for value in old:
                h, m, l = split3(value * sign)
                lhs = jnp.concatenate([h, h, m, h, l, m], axis=0)
                outs.append(lax.dot_general(lhs, rhs, (((0,), (0,)), ((), ())), preferred_element_type=F32))
            for i in range(2):
                at = slice(128 * i, 128 * i + 128)
                held = packed[i]
                if i == half:
                    held = jnp.where(inside, 0.0, held)
                packed[i] = held - jnp.where(lower, outs[0][:, at], outs[1][:, at])
                packed[i, rows] = new[i]
                if b + PANEL < 128:
                    packed[i, after] = ahead[i]
        mats[0, block, block], mats[1, block, block] = exchange(packed[0], packed[1])
        others = [slice(128 * i, 128 * i + 128) for i in ((k + 1) % 4, (k + 2) % 4, (k + 3) % 4)]
        for s in range(2):
            inverse = mats[s, block, block]
            rest = dot(inverse, jnp.concatenate([mats[s, block, at] for at in others], axis=1))
            left = jnp.concatenate([mats[s, at, block] for at in others], axis=0)
            out = dot(left, jnp.concatenate([inverse, rest], axis=1))
            for i, at_i in enumerate(others):
                here = slice(128 * i, 128 * i + 128)
                mats[s, block, at_i] = rest[:, here]
                mats[s, at_i, block] = -out[here, :128]
                for j, at_j in enumerate(others):
                    mats[s, at_i, at_j] = mats[s, at_i, at_j] - out[here, 128 * j + 128 : 128 * j + 256]


def pick_kernel(place, index, frames, residual, out, total, padded):
    step = pl.program_id(0)
    positions = place[2] + step * PICK + lax.broadcasted_iota(jnp.int32, (PICK, BLOCK), 0)
    padded[...] = jnp.zeros_like(padded)
    padded[:ROWS] = residual[...]
    parts = [v.astype(F32) for v in split3(padded[...])] + [jnp.zeros((8, PICK), F32)]
    packed = jnp.concatenate(
        [frames[...], jnp.zeros((16, PICK), BF16), jnp.concatenate(parts, axis=0).astype(BF16)], axis=0
    )
    picked = []
    for s in range(STEPS):
        select = jnp.where(index[s : s + 1] == positions, 1.0, 0.0).astype(BF16)
        picked.append(jnp.dot(packed, select, preferred_element_type=F32))

    @pl.when(step == 0)
    def _():
        for s in range(STEPS):
            total[s] = picked[s]

    @pl.when(step > 0)
    def _():
        for s in range(STEPS):
            total[s] += picked[s]

    @pl.when(step == pl.num_programs(0) - 1)
    def _():
        for s in range(STEPS):
            out[:, 32 * s : 32 * s + 32] = total[s].T.astype(BF16).reshape(16, 32, 256)


def pick(place, index, frames, residual):
    return pl.pallas_call(
        pick_kernel,
        grid=(frames.shape[1] // PICK,),
        in_specs=[
            pl.BlockSpec(memory_space=pltpu.SMEM),
            pl.BlockSpec(memory_space=pltpu.VMEM),
            pl.BlockSpec((112, PICK), lambda i: (0, i)),
            pl.BlockSpec((ROWS, PICK), lambda i: (0, i)),
        ],
        out_specs=pl.BlockSpec((16, 64, 256), lambda i: (0, 0, 0)),
        out_shape=jax.ShapeDtypeStruct((16, 64, 256), BF16),
        scratch_shapes=[pltpu.VMEM((STEPS, 256, BLOCK), F32), pltpu.VMEM((40, PICK), F32)],
        compiler_params=pltpu.CompilerParams(vmem_limit_bytes=60 << 20),
        name="pick",
    )(place, index, frames, residual)


def add_kernel(held, out):
    total = held[0].astype(F32)
    for i in range(1, 16):
        total = total + held[i].astype(F32)
    total = total.astype(BF16)
    for i in range(8):
        out[i] = total


def add(held):
    return pl.pallas_call(add_kernel, out_shape=jax.ShapeDtypeStruct((8, 64, 256), BF16), name="add")(held)


def mix_kernel(place, held, out):
    def total(at):
        value = held[at].astype(F32)
        for i in range(at + 1, at + 4):
            value = value + held[i].astype(F32)
        return value

    sums = total(0), total(4)
    first = place[0] == 0
    mine = jnp.where(first, sums[0], sums[1])
    other = pltpu.roll(jnp.where(first, sums[1], sums[0])[:, :128], 112, 1)
    lane = lax.broadcasted_iota(jnp.int32, (1, 128), 1)
    near = mine[:, :128] + jnp.where(lane >= 112, other, 0.0)
    tail = jnp.where(lane < 112, other, 0.0)
    value = jnp.concatenate([near, tail, mine[:, 128:]], axis=1).astype(BF16)
    for i in range(16):
        out[i] = value


def mix(place, held):
    return pl.pallas_call(
        mix_kernel,
        in_specs=[pl.BlockSpec(memory_space=pltpu.SMEM), pl.BlockSpec(memory_space=pltpu.VMEM)],
        out_shape=jax.ShapeDtypeStruct((16, 64, 384), BF16),
        name="mix",
    )(place, held)


def solve_kernel(near, far, point_row, point_col, delta_ref, sq_ref, mats, packed, grams):
    eye = lax.broadcasted_iota(jnp.int32, (BLOCK, BLOCK), 0) == lax.broadcasted_iota(jnp.int32, (BLOCK, BLOCK), 1)

    def columns(ref, s, at):
        return ref[:, 32 * s : 32 * s + 32, at].reshape(BLOCK, at.stop - at.start)

    def inner(a, b):
        total = 0.0
        for ref in (near, far):
            total = total + lax.dot_general(
                columns(ref, a, slice(0, 256)),
                columns(ref, b, slice(0, 256)),
                (((1,), (1,)), ((), ())),
                preferred_element_type=F32,
            )
        return total

    rows, cols = [], []
    for s in range(STEPS):
        products = inner(s, s)
        diagonal = jnp.where(eye, products, 0.0)
        rows.append(jnp.sum(diagonal, axis=0, keepdims=True))
        cols.append(jnp.sum(diagonal, axis=1, keepdims=True))
        sq_ref[BLOCK * s : BLOCK * s + BLOCK] = cols[s]
        kern = jnp.exp2(-SCALE * (cols[s] + rows[s] - 2.0 * products))
        mats[s] = grams[s] = kern + jnp.where(eye, RIDGE, 0.0)
    cross = jnp.exp2(-SCALE * (cols[0] + rows[1] - 2.0 * inner(0, 1)))
    cross = cross + jnp.where(point_col[...] == point_row[...], RIDGE, 0.0)
    lane = lax.broadcasted_iota(jnp.int32, (1, 128), 1)

    def block_res(s):
        both = []
        for ref in (near, far):
            part = [columns(ref, s, slice(256, 384)).astype(F32)]
            part.append(pltpu.roll(part[0], 128 - 40, 1))
            part.append(pltpu.roll(part[0], 128 - 80, 1))
            both.append(jnp.where(lane < 40, part[0] + (part[1] + part[2]), 0.0))
        return (both[0] + pltpu.roll(both[1], 64, 1)).T

    res = [block_res(s) for s in range(STEPS)]
    invert(mats, packed)
    for s in range(STEPS):
        if s == 1:
            res[1] = res[1] - dot_rows(delta, cross)
        delta = dot_rows(res[s], mats[s])
        delta = delta + dot_rows(res[s] - dot_rows(delta, grams[s]), mats[s])
        pad = jnp.zeros((8, BLOCK), F32)
        stacked = []
        for at in (0, 64):
            stacked += [v.astype(F32) for v in split3(delta[at : at + 40])] + [pad]
        delta_ref[:, BLOCK * s : BLOCK * s + BLOCK] = jnp.concatenate(stacked, axis=0).astype(BF16)


def solve(near, far, chosen):
    return pl.pallas_call(
        solve_kernel,
        out_shape=(
            jax.ShapeDtypeStruct((256, STEPS * BLOCK), BF16),
            jax.ShapeDtypeStruct((STEPS * BLOCK, 1), F32),
        ),
        scratch_shapes=[
            pltpu.VMEM((2, BLOCK, BLOCK), F32),
            pltpu.VMEM((2, 128, 128), F32),
            pltpu.VMEM((2, BLOCK, BLOCK), F32),
        ],
        compiler_params=pltpu.CompilerParams(vmem_limit_bytes=40 << 20),
        cost_estimate=pl.CostEstimate(flops=1 << 20, bytes_accessed=1 << 20, transcendentals=0),
        name="solve",
    )(near, far, chosen[1].reshape(1, BLOCK), chosen[0].reshape(BLOCK, 1))


def update_kernel(s0, s2, s3, a0, a1, a2, near, far, delta, sq, local, mine_ref, theirs_ref):
    s1 = jnp.where(pl.program_id(0) == 0, jnp.concatenate([a0[...], a1[...]], axis=1), a2[...])

    def squares(ref):
        value = ref[...].astype(F32)
        return jnp.sum(value * value, axis=0, keepdims=True)

    source_sq = SCALE * (squares(s0) + squares(s1) + squares(s2) + squares(s3))
    pad = jnp.zeros((32, TILE), BF16)
    source_near = jnp.concatenate([s0[...], s1, pad], axis=0)
    source_far = jnp.concatenate([s2[...], s3[...], pad], axis=0)
    positions = pl.program_id(0) * TILE + lax.broadcasted_iota(jnp.int32, (1, TILE), 1)
    change = jnp.zeros((256, TILE), F32)
    placed = jnp.zeros((256, TILE), F32)
    size = 512
    for c in range(STEPS * BLOCK // size):
        at = slice(size * c, size * c + size)
        s, first = (size * c) // BLOCK, (size * c) % BLOCK // 32
        block = slice(first, first + size // 32), slice(32 * s, 32 * s + 32), slice(0, 256)
        products = jnp.dot(near[block].reshape(size, 256), source_near, preferred_element_type=F32)
        products = products + jnp.dot(far[block].reshape(size, 256), source_far, preferred_element_type=F32)
        kern = jnp.exp2((2.0 * SCALE) * products - (SCALE * sq[at] + source_sq))
        here = jnp.where(local[at] == positions, 1.0, 0.0).astype(BF16)
        weights = delta[:, at]
        for part in split3(kern):
            change = change + jnp.dot(weights, part, preferred_element_type=F32)
        placed = placed + jnp.dot(weights, here, preferred_element_type=F32)
    for at, out in ((0, mine_ref), (128, theirs_ref)):
        moved = change[at : at + 40] + (change[at + 40 : at + 80] + change[at + 80 : at + 120])
        added = placed[at : at + 40] + (placed[at + 40 : at + 80] + placed[at + 80 : at + 120])
        out[0] = moved + RIDGE * added
        out[1] = added


def update(sources, across, near, far, delta, sq, local):
    whole = pl.BlockSpec(memory_space=pltpu.VMEM)
    rows = sources[0].shape[1]
    return pl.pallas_call(
        update_kernel,
        grid=(rows // TILE,),
        in_specs=[pl.BlockSpec((112, TILE), lambda i: (0, i))] * 3 + [whole] * 8,
        out_specs=[pl.BlockSpec((2, 40, TILE), lambda i: (0, 0, i))] * 2,
        out_shape=[jax.ShapeDtypeStruct((2, 40, rows), F32)] * 2,
        compiler_params=pltpu.CompilerParams(vmem_limit_bytes=40 << 20),
        name="update",
    )(*sources, *across, near, far, delta, sq, local)


def finish_kernel(place, residual, coefficients, mine, got, res_out, coef_out):
    own = pl.program_id(0) == place[1]
    value = jnp.where(own, mine[...], got[...])
    res_out[...] = residual[...] - value[0, :ROWS]
    coef_out[...] = coefficients[...] + value[1, :ROWS]


def finish(place, residual, coefficients, mine, got):
    whole = pl.BlockSpec(memory_space=pltpu.VMEM)
    half = pl.BlockSpec((ROWS, residual.shape[1] // 2), lambda i: (0, i))
    return pl.pallas_call(
        finish_kernel,
        grid=(2,),
        in_specs=[pl.BlockSpec(memory_space=pltpu.SMEM), half, half, whole, whole],
        out_specs=[half, half],
        out_shape=[jax.ShapeDtypeStruct(residual.shape, F32)] * 2,
        compiler_params=pltpu.CompilerParams(vmem_limit_bytes=40 << 20),
        name="finish",
    )(place, residual, coefficients, mine, got)


def on_device(frames, residual, coefficients, block_index):
    rows = frames.shape[1]
    dp, feat = lax.axis_index("dp"), lax.axis_index("feat")
    h, c = feat // 2, feat % 2
    place = jnp.stack([h, c, dp * rows]).astype(jnp.int32)
    own_half = lax.dynamic_slice_in_dim(frames, c * (rows // 2), rows // 2, axis=1)
    other_half = lax.dynamic_slice_in_dim(frames, (1 - c) * (rows // 2), rows // 2, axis=1)
    beside = swap(other_half, 0, 1)
    size = rows // 8
    own = [own_half[:, :size], own_half[:, size : 2 * size], own_half[:, 2 * size :]]
    across = [swap(own[0], 1, 0)]

    held = pick(place, block_index, frames, residual)
    held = add(lax.all_to_all(held, "dp", 0, 0, axis_index_groups=PLANE, tiled=True))
    held, beside, across, own, other_half = lax.optimization_barrier((held, beside, across, own, other_half))
    held = lax.all_to_all(held, AXES, 0, 0, axis_index_groups=LINE, tiled=True)
    held, own, other_half = lax.optimization_barrier((held, own, other_half))
    across.append(swap(own[1], 1, 0))
    near = lax.all_to_all(mix(place, held), "dp", 0, 0, axis_index_groups=PLANE, tiled=True)
    near, across, own, other_half = lax.optimization_barrier((near, across, own, other_half))
    far = swap(near, 0, 1)
    across.append(swap(own[2], 1, 0))
    diagonal = swap(other_half, 1, 1)

    delta, sq = solve(near, far, block_index)
    local = block_index.reshape(-1, 1) - dp * rows - c * (rows // 2)
    mine, theirs = update((own_half, beside, diagonal), across, near, far, delta, sq, local)
    return finish(place, residual, coefficients, mine, swap(theirs, 0, 1))


def solution(mesh):
    return jax.shard_map(
        on_device,
        mesh=mesh,
        in_specs=(P("feat", "dp"), P("feat", "dp"), P("feat", "dp"), P()),
        out_specs=(P("feat", "dp"), P("feat", "dp")),
        check_vma=False,
    )
```

```python
import functools
import math

import jax
import jax.numpy as jnp
from jax import lax
from jax.experimental import pallas as pl
from jax.experimental.pallas import tpu as pltpu
from jax.sharding import PartitionSpec as P

D = 448
STEPS = 2
BLOCK = 512
RIDGE = 0.1
WIDTH_SCALE = 2.0
AXES = ("dp", "feat")
BF16 = jnp.bfloat16
F32 = jnp.float32
ROWS = 37
PANEL = 16
TILE = 1024
PICK = 1024
SCALE = WIDTH_SCALE / D * math.log2(math.e)


def permutation(move):
    pairs = []
    for d in range(64):
        for g in range(4):
            y, x, z, h, c = move(d // 16, (d // 4) % 4, d % 4, g // 2, g % 2)
            pairs.append((d * 4 + g, ((y % 4) * 16 + (x % 4) * 4 + z % 4) * 4 + (h % 2) * 2 + c % 2))
    return pairs


def swap(value, dh, dc):
    def move(y, x, z, h, c):
        return y, x, z, h + dh, c + dc

    return lax.ppermute(value, AXES, permutation(move))


PLANE = [[r * 4 + z for r in range(16)] for z in range(4)]
LINE = [[(r * 4 + z) * 4 + h * 2 + c for h in range(2) for z in range(4)] for r in range(16) for c in range(2)]


def split3(value):
    high = value.astype(BF16)
    rest = value - high.astype(F32)
    mid = rest.astype(BF16)
    low = (rest - mid.astype(F32)).astype(BF16)
    return high, mid, low


def dot(a, b):
    ah, am, al = split3(a)
    bh, bm, bl = split3(b)
    lhs = jnp.concatenate([al, ah, am, am, ah, ah], axis=1)
    rhs = jnp.concatenate([bh, bl, bm, bh, bm, bh], axis=0)
    return jnp.dot(lhs, rhs, preferred_element_type=F32)


def dot_rows(a, b):
    ah, am, al = split3(a)
    n = a.shape[0]
    total = 0.0
    for value, lhs in zip(reversed(split3(b)), ((ah,), (am, ah), (al, am, ah))):
        out = jnp.dot(jnp.concatenate(lhs, axis=0), value, preferred_element_type=F32)
        for i in range(len(lhs)):
            total = total + out[n * i : n * i + n]
    return total


def invert(mats, packed):
    lane = lax.broadcasted_iota(jnp.int32, (1, 128), 1)
    lower = lane < 64
    row = lax.broadcasted_iota(jnp.int32, (PANEL, 128), 0)

    def exchange(one, two):
        return jnp.where(lower, one, pltpu.roll(two, 64, 1)), jnp.where(lower, pltpu.roll(one, 64, 1), two)

    def spread(value, first):
        pairs = [[jnp.broadcast_to(value[:, i : i + 1], (PANEL, 128)) for i in (j, 64 + j)] for j in range(first, first + PANEL)]
        return [jnp.where(lower, *pair) for pair in pairs]

    for k in range(4):
        r0 = 128 * k
        block = slice(r0, r0 + 128)
        packed[0], packed[1] = exchange(mats[0, block, block], mats[1, block, block])
        ahead = [packed[0, :PANEL], packed[1, :PANEL]]
        for p in range(128 // PANEL):
            b = PANEL * p
            half, first = b // 64, b % 64
            rows, after = slice(b, b + PANEL), slice(b + PANEL, b + 2 * PANEL)
            inside = ((lane & 63) >= first) & ((lane & 63) < first + PANEL)
            new = ahead
            old = exchange(*new)
            cols = spread(new[half], first)
            if b + PANEL < 128:
                ahead = [packed[0, after], packed[1, after]]
                left = spread(ahead[half], first)
                ahead[half] = jnp.where(inside, 0.0, ahead[half])
            for j in range(PANEL):
                one = jnp.where(row == j, 1.0, 0.0)
                factor = (cols[j] - one) * (1.0 / cols[j][j : j + 1])
                for q in range(j + 1, PANEL):
                    cols[q] = cols[q] - factor * cols[q][j : j + 1]
                new[half] = jnp.where((lane & 63) == first + j, one, new[half])
                new = [value - factor * value[j : j + 1] for value in new]
            if b + PANEL < 128:
                for j in range(PANEL):
                    ahead = [value - left[j] * add[j : j + 1] for value, add in zip(ahead, new)]
            sign = jnp.where(lane < b, -1.0, jnp.where(lane < b + PANEL, 0.0, 1.0))
            nh, nm, nl = split3(jnp.concatenate(new, axis=1))
            rhs = jnp.concatenate([nh, nm, nh, nl, nh, nm], axis=0)
            outs = []
            for value in old:
                h, m, l = split3(value * sign)
                lhs = jnp.concatenate([h, h, m, h, l, m], axis=0)
                outs.append(lax.dot_general(lhs, rhs, (((0,), (0,)), ((), ())), preferred_element_type=F32))
            for i in range(2):
                at = slice(128 * i, 128 * i + 128)
                held = packed[i]
                if i == half:
                    held = jnp.where(inside, 0.0, held)
                packed[i] = held - jnp.where(lower, outs[0][:, at], outs[1][:, at])
                packed[i, rows] = new[i]
                if b + PANEL < 128:
                    packed[i, after] = ahead[i]
        mats[0, block, block], mats[1, block, block] = exchange(packed[0], packed[1])
        others = [slice(128 * i, 128 * i + 128) for i in ((k + 1) % 4, (k + 2) % 4, (k + 3) % 4)]
        for s in range(2):
            inverse = mats[s, block, block]
            rest = dot(inverse, jnp.concatenate([mats[s, block, at] for at in others], axis=1))
            left = jnp.concatenate([mats[s, at, block] for at in others], axis=0)
            out = dot(left, jnp.concatenate([inverse, rest], axis=1))
            for i, at_i in enumerate(others):
                here = slice(128 * i, 128 * i + 128)
                mats[s, block, at_i] = rest[:, here]
                mats[s, at_i, block] = -out[here, :128]
                for j, at_j in enumerate(others):
                    mats[s, at_i, at_j] = mats[s, at_i, at_j] - out[here, 128 * j + 128 : 128 * j + 256]


def pick_kernel(place, index, frames, residual, out, total, padded):
    step = pl.program_id(0)
    positions = place[2] + step * PICK + lax.broadcasted_iota(jnp.int32, (PICK, BLOCK), 0)
    padded[...] = jnp.zeros_like(padded)
    padded[:ROWS] = residual[...]
    parts = [v.astype(F32) for v in split3(padded[...])] + [jnp.zeros((8, PICK), F32)]
    packed = jnp.concatenate(
        [frames[...], jnp.zeros((16, PICK), BF16), jnp.concatenate(parts, axis=0).astype(BF16)], axis=0
    )
    picked = []
    for s in range(STEPS):
        select = jnp.where(index[s : s + 1] == positions, 1.0, 0.0).astype(BF16)
        picked.append(jnp.dot(packed, select, preferred_element_type=F32))

    @pl.when(step == 0)
    def _():
        for s in range(STEPS):
            total[s] = picked[s]

    @pl.when(step > 0)
    def _():
        for s in range(STEPS):
            total[s] += picked[s]

    @pl.when(step == pl.num_programs(0) - 1)
    def _():
        for s in range(STEPS):
            out[:, 32 * s : 32 * s + 32] = total[s].T.astype(BF16).reshape(16, 32, 256)


def pick(place, index, frames, residual):
    return pl.pallas_call(
        pick_kernel,
        grid=(frames.shape[1] // PICK,),
        in_specs=[
            pl.BlockSpec(memory_space=pltpu.SMEM),
            pl.BlockSpec(memory_space=pltpu.VMEM),
            pl.BlockSpec((112, PICK), lambda i: (0, i)),
            pl.BlockSpec((ROWS, PICK), lambda i: (0, i)),
        ],
        out_specs=pl.BlockSpec((16, 64, 256), lambda i: (0, 0, 0)),
        out_shape=jax.ShapeDtypeStruct((16, 64, 256), BF16),
        scratch_shapes=[pltpu.VMEM((STEPS, 256, BLOCK), F32), pltpu.VMEM((40, PICK), F32)],
        compiler_params=pltpu.CompilerParams(vmem_limit_bytes=60 << 20),
        name="pick",
    )(place, index, frames, residual)


def add_kernel(held, out):
    total = held[0].astype(F32)
    for i in range(1, 16):
        total = total + held[i].astype(F32)
    total = total.astype(BF16)
    for i in range(8):
        out[i] = total


def add(held):
    return pl.pallas_call(add_kernel, out_shape=jax.ShapeDtypeStruct((8, 64, 256), BF16), name="add")(held)


def mix_kernel(place, held, out):
    def total(at):
        value = held[at].astype(F32)
        for i in range(at + 1, at + 4):
            value = value + held[i].astype(F32)
        return value

    sums = total(0), total(4)
    first = place[0] == 0
    mine = jnp.where(first, sums[0], sums[1])
    other = pltpu.roll(jnp.where(first, sums[1], sums[0])[:, :128], 112, 1)
    lane = lax.broadcasted_iota(jnp.int32, (1, 128), 1)
    near = mine[:, :128] + jnp.where(lane >= 112, other, 0.0)
    tail = jnp.where(lane < 112, other, 0.0)
    value = jnp.concatenate([near, tail, mine[:, 128:]], axis=1).astype(BF16)
    for i in range(16):
        out[i] = value


def mix(place, held):
    return pl.pallas_call(
        mix_kernel,
        in_specs=[pl.BlockSpec(memory_space=pltpu.SMEM), pl.BlockSpec(memory_space=pltpu.VMEM)],
        out_shape=jax.ShapeDtypeStruct((16, 64, 384), BF16),
        name="mix",
    )(place, held)


def solve_kernel(near, far, point_row, point_col, delta_ref, sq_ref, mats, packed, grams):
    eye = lax.broadcasted_iota(jnp.int32, (BLOCK, BLOCK), 0) == lax.broadcasted_iota(jnp.int32, (BLOCK, BLOCK), 1)

    def columns(ref, s, at):
        return ref[:, 32 * s : 32 * s + 32, at].reshape(BLOCK, at.stop - at.start)

    def inner(a, b):
        total = 0.0
        for ref in (near, far):
            total = total + lax.dot_general(
                columns(ref, a, slice(0, 256)),
                columns(ref, b, slice(0, 256)),
                (((1,), (1,)), ((), ())),
                preferred_element_type=F32,
            )
        return total

    rows, cols = [], []
    for s in range(STEPS):
        products = inner(s, s)
        diagonal = jnp.where(eye, products, 0.0)
        rows.append(jnp.sum(diagonal, axis=0, keepdims=True))
        cols.append(jnp.sum(diagonal, axis=1, keepdims=True))
        sq_ref[BLOCK * s : BLOCK * s + BLOCK] = cols[s]
        kern = jnp.exp2(-SCALE * (cols[s] + rows[s] - 2.0 * products))
        mats[s] = grams[s] = kern + jnp.where(eye, RIDGE, 0.0)
    cross = jnp.exp2(-SCALE * (cols[0] + rows[1] - 2.0 * inner(0, 1)))
    cross = cross + jnp.where(point_col[...] == point_row[...], RIDGE, 0.0)
    lane = lax.broadcasted_iota(jnp.int32, (1, 128), 1)

    def block_res(s):
        both = []
        for ref in (near, far):
            part = [columns(ref, s, slice(256, 384)).astype(F32)]
            part.append(pltpu.roll(part[0], 128 - 40, 1))
            part.append(pltpu.roll(part[0], 128 - 80, 1))
            both.append(jnp.where(lane < 40, part[0] + (part[1] + part[2]), 0.0))
        return (both[0] + pltpu.roll(both[1], 64, 1)).T

    res = [block_res(s) for s in range(STEPS)]
    invert(mats, packed)
    for s in range(STEPS):
        if s == 1:
            res[1] = res[1] - dot_rows(delta, cross)
        delta = dot_rows(res[s], mats[s])
        delta = delta + dot_rows(res[s] - dot_rows(delta, grams[s]), mats[s])
        pad = jnp.zeros((8, BLOCK), F32)
        stacked = []
        for at in (0, 64):
            stacked += [v.astype(F32) for v in split3(delta[at : at + 40])] + [pad]
        delta_ref[:, BLOCK * s : BLOCK * s + BLOCK] = jnp.concatenate(stacked, axis=0).astype(BF16)


def solve(near, far, chosen):
    return pl.pallas_call(
        solve_kernel,
        out_shape=(
            jax.ShapeDtypeStruct((256, STEPS * BLOCK), BF16),
            jax.ShapeDtypeStruct((STEPS * BLOCK, 1), F32),
        ),
        scratch_shapes=[
            pltpu.VMEM((2, BLOCK, BLOCK), F32),
            pltpu.VMEM((2, 128, 128), F32),
            pltpu.VMEM((2, BLOCK, BLOCK), F32),
        ],
        compiler_params=pltpu.CompilerParams(vmem_limit_bytes=40 << 20),
        cost_estimate=pl.CostEstimate(flops=1 << 20, bytes_accessed=1 << 20, transcendentals=0),
        name="solve",
    )(near, far, chosen[1].reshape(1, BLOCK), chosen[0].reshape(BLOCK, 1))


def update_kernel(part, s0, s2, s3, *refs):
    *across, near, far, delta, sq, local, mine_ref, theirs_ref = refs
    s1 = across[0][...] if len(across) == 1 else jnp.concatenate([one[...] for one in across], axis=1)

    def squares(ref):
        value = ref[...].astype(F32)
        return jnp.sum(value * value, axis=0, keepdims=True)

    source_sq = SCALE * (squares(s0) + squares(s1) + squares(s2) + squares(s3))
    pad = jnp.zeros((32, TILE), BF16)
    source_near = jnp.concatenate([s0[...], s1, pad], axis=0)
    source_far = jnp.concatenate([s2[...], s3[...], pad], axis=0)
    positions = part * TILE + lax.broadcasted_iota(jnp.int32, (1, TILE), 1)
    change = jnp.zeros((256, TILE), F32)
    placed = jnp.zeros((256, TILE), F32)
    size = 512
    for c in range(STEPS * BLOCK // size):
        at = slice(size * c, size * c + size)
        s, first = (size * c) // BLOCK, (size * c) % BLOCK // 32
        block = slice(first, first + size // 32), slice(32 * s, 32 * s + 32), slice(0, 256)
        products = jnp.dot(near[block].reshape(size, 256), source_near, preferred_element_type=F32)
        products = products + jnp.dot(far[block].reshape(size, 256), source_far, preferred_element_type=F32)
        kern = jnp.exp2((2.0 * SCALE) * products - (SCALE * sq[at] + source_sq))
        here = jnp.where(local[at] == positions, 1.0, 0.0).astype(BF16)
        weights = delta[:, at]
        for part in split3(kern):
            change = change + jnp.dot(weights, part, preferred_element_type=F32)
        placed = placed + jnp.dot(weights, here, preferred_element_type=F32)
    for at, out in ((0, mine_ref), (128, theirs_ref)):
        moved = change[at : at + 40] + (change[at + 40 : at + 80] + change[at + 80 : at + 120])
        added = placed[at : at + 40] + (placed[at + 40 : at + 80] + placed[at + 80 : at + 120])
        out[0] = moved + RIDGE * added
        out[1] = added


def update(part, sources, across, near, far, delta, sq, local):
    whole = pl.BlockSpec(memory_space=pltpu.VMEM)
    return pl.pallas_call(
        functools.partial(update_kernel, part),
        grid=(1,),
        in_specs=[pl.BlockSpec((112, TILE), lambda i: (0, part))] * 3 + [whole] * (len(across) + 5),
        out_specs=[whole] * 2,
        out_shape=[jax.ShapeDtypeStruct((2, 40, TILE), F32)] * 2,
        compiler_params=pltpu.CompilerParams(vmem_limit_bytes=40 << 20),
        name="update",
    )(*sources, *across, near, far, delta, sq, local)


def finish_kernel(place, residual, coefficients, mine0, mine1, got0, got1, res_out, coef_out):
    own = pl.program_id(0) == place[1]
    for i, (mine, got) in enumerate(((mine0, got0), (mine1, got1))):
        at = slice(TILE * i, TILE * i + TILE)
        value = jnp.where(own, mine[...], got[...])
        res_out[:, at] = residual[:, at] - value[0, :ROWS]
        coef_out[:, at] = coefficients[:, at] + value[1, :ROWS]


def finish(place, residual, coefficients, *parts):
    whole = pl.BlockSpec(memory_space=pltpu.VMEM)
    half = pl.BlockSpec((ROWS, residual.shape[1] // 2), lambda i: (0, i))
    return pl.pallas_call(
        finish_kernel,
        grid=(2,),
        in_specs=[pl.BlockSpec(memory_space=pltpu.SMEM), half, half] + [whole] * 4,
        out_specs=[half, half],
        out_shape=[jax.ShapeDtypeStruct(residual.shape, F32)] * 2,
        compiler_params=pltpu.CompilerParams(vmem_limit_bytes=40 << 20),
        name="finish",
    )(place, residual, coefficients, *parts)


def on_device(frames, residual, coefficients, block_index):
    rows = frames.shape[1]
    dp, feat = lax.axis_index("dp"), lax.axis_index("feat")
    h, c = feat // 2, feat % 2
    place = jnp.stack([h, c, dp * rows]).astype(jnp.int32)
    own_half = lax.dynamic_slice_in_dim(frames, c * (rows // 2), rows // 2, axis=1)
    other_half = lax.dynamic_slice_in_dim(frames, (1 - c) * (rows // 2), rows // 2, axis=1)
    beside = swap(other_half, 0, 1)
    size = rows // 8
    own = [own_half[:, :size], own_half[:, size : 2 * size], own_half[:, 2 * size :]]
    across = [swap(own[0], 1, 0)]

    held = pick(place, block_index, frames, residual)
    held = add(lax.all_to_all(held, "dp", 0, 0, axis_index_groups=PLANE, tiled=True))
    held, beside, across, own, other_half = lax.optimization_barrier((held, beside, across, own, other_half))
    held = lax.all_to_all(held, AXES, 0, 0, axis_index_groups=LINE, tiled=True)
    held, own, other_half = lax.optimization_barrier((held, own, other_half))
    across.append(swap(own[1], 1, 0))
    near = lax.all_to_all(mix(place, held), "dp", 0, 0, axis_index_groups=PLANE, tiled=True)
    near, across, own, other_half = lax.optimization_barrier((near, across, own, other_half))
    far = swap(near, 0, 1)
    across.append(swap(own[2], 1, 0))
    diagonal = swap(other_half, 1, 1)

    delta, sq = solve(near, far, block_index)
    local = block_index.reshape(-1, 1) - dp * rows - c * (rows // 2)
    sources = own_half, beside, diagonal
    mine0, theirs0 = update(0, sources, across[:2], near, far, delta, sq, local)
    near, mine0, theirs0 = lax.optimization_barrier((near, mine0, theirs0))
    got0 = swap(theirs0, 0, 1)
    mine1, theirs1 = update(1, sources, across[2:], near, far, delta, sq, local)
    got1 = swap(theirs1, 0, 1)
    return finish(place, residual, coefficients, mine0, mine1, got0, got1)


def solution(mesh):
    return jax.shard_map(
        on_device,
        mesh=mesh,
        in_specs=(P("feat", "dp"), P("feat", "dp"), P("feat", "dp"), P()),
        out_specs=(P("feat", "dp"), P("feat", "dp")),
        check_vma=False,
    )
```

```python
import functools
import math

import jax
import jax.numpy as jnp
from jax import lax
from jax.experimental import pallas as pl
from jax.experimental.pallas import tpu as pltpu
from jax.sharding import PartitionSpec as P

D = 448
STEPS = 2
BLOCK = 512
RIDGE = 0.1
WIDTH_SCALE = 2.0
AXES = ("dp", "feat")
BF16 = jnp.bfloat16
F32 = jnp.float32
ROWS = 37
PANEL = 16
TILE = 1024
PICK = 1024
SCALE = WIDTH_SCALE / D * math.log2(math.e)


def permutation(move):
    pairs = []
    for d in range(64):
        for g in range(4):
            y, x, z, h, c = move(d // 16, (d // 4) % 4, d % 4, g // 2, g % 2)
            pairs.append((d * 4 + g, ((y % 4) * 16 + (x % 4) * 4 + z % 4) * 4 + (h % 2) * 2 + c % 2))
    return pairs


def swap(value, dh, dc):
    def move(y, x, z, h, c):
        return y, x, z, h + dh, c + dc

    return lax.ppermute(value, AXES, permutation(move))


PLANE = [[r * 4 + z for r in range(16)] for z in range(4)]
LINE = [[(r * 4 + z) * 4 + h * 2 + c for h in range(2) for z in range(4)] for r in range(16) for c in range(2)]


def split3(value):
    high = value.astype(BF16)
    rest = value - high.astype(F32)
    mid = rest.astype(BF16)
    low = (rest - mid.astype(F32)).astype(BF16)
    return high, mid, low


def dot(a, b):
    ah, am, al = split3(a)
    bh, bm, bl = split3(b)
    lhs = jnp.concatenate([al, ah, am, am, ah, ah], axis=1)
    rhs = jnp.concatenate([bh, bl, bm, bh, bm, bh], axis=0)
    return jnp.dot(lhs, rhs, preferred_element_type=F32)


def dot_rows(a, b):
    ah, am, al = split3(a)
    n = a.shape[0]
    total = 0.0
    for value, lhs in zip(reversed(split3(b)), ((ah,), (am, ah), (al, am, ah))):
        out = jnp.dot(jnp.concatenate(lhs, axis=0), value, preferred_element_type=F32)
        for i in range(len(lhs)):
            total = total + out[n * i : n * i + n]
    return total


def invert(mats, packed):
    lane = lax.broadcasted_iota(jnp.int32, (1, 128), 1)
    lower = lane < 64
    row = lax.broadcasted_iota(jnp.int32, (PANEL, 128), 0)

    def exchange(one, two):
        return jnp.where(lower, one, pltpu.roll(two, 64, 1)), jnp.where(lower, pltpu.roll(one, 64, 1), two)

    def spread(value, first):
        pairs = [[jnp.broadcast_to(value[:, i : i + 1], (PANEL, 128)) for i in (j, 64 + j)] for j in range(first, first + PANEL)]
        return [jnp.where(lower, *pair) for pair in pairs]

    for k in range(4):
        r0 = 128 * k
        block = slice(r0, r0 + 128)
        packed[0], packed[1] = exchange(mats[0, block, block], mats[1, block, block])
        ahead = [packed[0, :PANEL], packed[1, :PANEL]]
        for p in range(128 // PANEL):
            b = PANEL * p
            half, first = b // 64, b % 64
            rows, after = slice(b, b + PANEL), slice(b + PANEL, b + 2 * PANEL)
            inside = ((lane & 63) >= first) & ((lane & 63) < first + PANEL)
            new = ahead
            old = exchange(*new)
            cols = spread(new[half], first)
            if b + PANEL < 128:
                ahead = [packed[0, after], packed[1, after]]
                left = spread(ahead[half], first)
                ahead[half] = jnp.where(inside, 0.0, ahead[half])
            for j in range(PANEL):
                one = jnp.where(row == j, 1.0, 0.0)
                factor = (cols[j] - one) * (1.0 / cols[j][j : j + 1])
                for q in range(j + 1, PANEL):
                    cols[q] = cols[q] - factor * cols[q][j : j + 1]
                new[half] = jnp.where((lane & 63) == first + j, one, new[half])
                new = [value - factor * value[j : j + 1] for value in new]
            if b + PANEL < 128:
                for j in range(PANEL):
                    ahead = [value - left[j] * add[j : j + 1] for value, add in zip(ahead, new)]
            sign = jnp.where(lane < b, -1.0, jnp.where(lane < b + PANEL, 0.0, 1.0))
            nh, nm, nl = split3(jnp.concatenate(new, axis=1))
            rhs = jnp.concatenate([nh, nm, nh, nl, nh, nm], axis=0)
            outs = []
            for value in old:
                h, m, l = split3(value * sign)
                lhs = jnp.concatenate([h, h, m, h, l, m], axis=0)
                outs.append(lax.dot_general(lhs, rhs, (((0,), (0,)), ((), ())), preferred_element_type=F32))
            for i in range(2):
                at = slice(128 * i, 128 * i + 128)
                held = packed[i]
                if i == half:
                    held = jnp.where(inside, 0.0, held)
                packed[i] = held - jnp.where(lower, outs[0][:, at], outs[1][:, at])
                packed[i, rows] = new[i]
                if b + PANEL < 128:
                    packed[i, after] = ahead[i]
        mats[0, block, block], mats[1, block, block] = exchange(packed[0], packed[1])
        others = [slice(128 * i, 128 * i + 128) for i in ((k + 1) % 4, (k + 2) % 4, (k + 3) % 4)]
        for s in range(2):
            inverse = mats[s, block, block]
            rest = dot(inverse, jnp.concatenate([mats[s, block, at] for at in others], axis=1))
            left = jnp.concatenate([mats[s, at, block] for at in others], axis=0)
            out = dot(left, jnp.concatenate([inverse, rest], axis=1))
            for i, at_i in enumerate(others):
                here = slice(128 * i, 128 * i + 128)
                mats[s, block, at_i] = rest[:, here]
                mats[s, at_i, block] = -out[here, :128]
                for j, at_j in enumerate(others):
                    mats[s, at_i, at_j] = mats[s, at_i, at_j] - out[here, 128 * j + 128 : 128 * j + 256]


def pick_kernel(place, index, frames, residual, out, total, padded):
    step = pl.program_id(0)
    positions = place[2] + step * PICK + lax.broadcasted_iota(jnp.int32, (PICK, BLOCK), 0)
    padded[...] = jnp.zeros_like(padded)
    padded[:ROWS] = residual[...]
    parts = [v.astype(F32) for v in split3(padded[...])] + [jnp.zeros((8, PICK), F32)]
    packed = jnp.concatenate(
        [frames[...], jnp.zeros((16, PICK), BF16), jnp.concatenate(parts, axis=0).astype(BF16)], axis=0
    )
    picked = []
    for s in range(STEPS):
        select = jnp.where(index[s : s + 1] == positions, 1.0, 0.0).astype(BF16)
        picked.append(jnp.dot(packed, select, preferred_element_type=F32))

    @pl.when(step == 0)
    def _():
        for s in range(STEPS):
            total[s] = picked[s]

    @pl.when(step > 0)
    def _():
        for s in range(STEPS):
            total[s] += picked[s]

    @pl.when(step == pl.num_programs(0) - 1)
    def _():
        for s in range(STEPS):
            out[:, 32 * s : 32 * s + 32] = total[s].T.astype(BF16).reshape(16, 32, 256)


def pick(place, index, frames, residual):
    return pl.pallas_call(
        pick_kernel,
        grid=(frames.shape[1] // PICK,),
        in_specs=[
            pl.BlockSpec(memory_space=pltpu.SMEM),
            pl.BlockSpec(memory_space=pltpu.VMEM),
            pl.BlockSpec((112, PICK), lambda i: (0, i)),
            pl.BlockSpec((ROWS, PICK), lambda i: (0, i)),
        ],
        out_specs=pl.BlockSpec((16, 64, 256), lambda i: (0, 0, 0)),
        out_shape=jax.ShapeDtypeStruct((16, 64, 256), BF16),
        scratch_shapes=[pltpu.VMEM((STEPS, 256, BLOCK), F32), pltpu.VMEM((40, PICK), F32)],
        compiler_params=pltpu.CompilerParams(vmem_limit_bytes=60 << 20),
        name="pick",
    )(place, index, frames, residual)


def add_kernel(held, out):
    total = held[0].astype(F32)
    for i in range(1, 16):
        total = total + held[i].astype(F32)
    total = total.astype(BF16)
    for i in range(8):
        out[i] = total


def add(held):
    return pl.pallas_call(add_kernel, out_shape=jax.ShapeDtypeStruct((8, 64, 256), BF16), name="add")(held)


def mix_kernel(place, held, out):
    def total(at):
        value = held[at].astype(F32)
        for i in range(at + 1, at + 4):
            value = value + held[i].astype(F32)
        return value

    sums = total(0), total(4)
    first = place[0] == 0
    mine = jnp.where(first, sums[0], sums[1])
    other = pltpu.roll(jnp.where(first, sums[1], sums[0])[:, :128], 112, 1)
    lane = lax.broadcasted_iota(jnp.int32, (1, 128), 1)
    near = mine[:, :128] + jnp.where(lane >= 112, other, 0.0)
    tail = jnp.where(lane < 112, other, 0.0)
    value = jnp.concatenate([near, tail, mine[:, 128:]], axis=1).astype(BF16)
    for i in range(16):
        out[i] = value


def mix(place, held):
    return pl.pallas_call(
        mix_kernel,
        in_specs=[pl.BlockSpec(memory_space=pltpu.SMEM), pl.BlockSpec(memory_space=pltpu.VMEM)],
        out_shape=jax.ShapeDtypeStruct((16, 64, 384), BF16),
        name="mix",
    )(place, held)


def solve_kernel(near, far, index, delta_ref, sq_ref, index_ref, mats, packed, grams):
    eye = lax.broadcasted_iota(jnp.int32, (BLOCK, BLOCK), 0) == lax.broadcasted_iota(jnp.int32, (BLOCK, BLOCK), 1)

    def columns(ref, s, at):
        return ref[:, 32 * s : 32 * s + 32, at].reshape(BLOCK, at.stop - at.start)

    def inner(a, b):
        total = 0.0
        for ref in (near, far):
            total = total + lax.dot_general(
                columns(ref, a, slice(0, 256)),
                columns(ref, b, slice(0, 256)),
                (((1,), (1,)), ((), ())),
                preferred_element_type=F32,
            )
        return total

    rows, cols, points = [], [], []
    for s in range(STEPS):
        products = inner(s, s)
        diagonal = jnp.where(eye, products, 0.0)
        rows.append(jnp.sum(diagonal, axis=0, keepdims=True))
        cols.append(jnp.sum(diagonal, axis=1, keepdims=True))
        sq_ref[BLOCK * s : BLOCK * s + BLOCK] = cols[s]
        points.append(jnp.broadcast_to(index[s : s + 1].astype(F32), (128, BLOCK)))
        index_ref[BLOCK * s : BLOCK * s + BLOCK] = points[s].T[:, :1]
        kern = jnp.exp2(-SCALE * (cols[s] + rows[s] - 2.0 * products))
        mats[s] = grams[s] = kern + jnp.where(eye, RIDGE, 0.0)
    cross = jnp.exp2(-SCALE * (cols[0] + rows[1] - 2.0 * inner(0, 1)))
    cross = cross + jnp.where(points[0].T[:, :1] == points[1][:1], RIDGE, 0.0)
    lane = lax.broadcasted_iota(jnp.int32, (1, 128), 1)

    def block_res(s):
        both = []
        for ref in (near, far):
            part = [columns(ref, s, slice(256, 384)).astype(F32)]
            part.append(pltpu.roll(part[0], 128 - 40, 1))
            part.append(pltpu.roll(part[0], 128 - 80, 1))
            both.append(jnp.where(lane < 40, part[0] + (part[1] + part[2]), 0.0))
        return (both[0] + pltpu.roll(both[1], 64, 1)).T

    res = [block_res(s) for s in range(STEPS)]
    invert(mats, packed)
    for s in range(STEPS):
        if s == 1:
            res[1] = res[1] - dot_rows(delta, cross)
        delta = dot_rows(res[s], mats[s])
        delta = delta + dot_rows(res[s] - dot_rows(delta, grams[s]), mats[s])
        pad = jnp.zeros((8, BLOCK), F32)
        stacked = []
        for at in (0, 64):
            stacked += [v.astype(F32) for v in split3(delta[at : at + 40])] + [pad]
        delta_ref[:, BLOCK * s : BLOCK * s + BLOCK] = jnp.concatenate(stacked, axis=0).astype(BF16)


def solve(near, far, chosen):
    return pl.pallas_call(
        solve_kernel,
        out_shape=(
            jax.ShapeDtypeStruct((256, STEPS * BLOCK), BF16),
            jax.ShapeDtypeStruct((STEPS * BLOCK, 1), F32),
            jax.ShapeDtypeStruct((STEPS * BLOCK, 1), F32),
        ),
        scratch_shapes=[
            pltpu.VMEM((2, BLOCK, BLOCK), F32),
            pltpu.VMEM((2, 128, 128), F32),
            pltpu.VMEM((2, BLOCK, BLOCK), F32),
        ],
        compiler_params=pltpu.CompilerParams(vmem_limit_bytes=40 << 20),
        cost_estimate=pl.CostEstimate(flops=1 << 20, bytes_accessed=1 << 20, transcendentals=0),
        name="solve",
    )(near, far, chosen)


def update_kernel(part, place, s0, s2, s3, *refs):
    *across, near, far, delta, sq, local, mine_ref, theirs_ref = refs
    s1 = across[0][...] if len(across) == 1 else jnp.concatenate([one[...] for one in across], axis=1)

    def squares(ref):
        value = ref[...].astype(F32)
        return jnp.sum(value * value, axis=0, keepdims=True)

    source_sq = SCALE * (squares(s0) + squares(s1) + squares(s2) + squares(s3))
    pad = jnp.zeros((32, TILE), BF16)
    source_near = jnp.concatenate([s0[...], s1, pad], axis=0)
    source_far = jnp.concatenate([s2[...], s3[...], pad], axis=0)
    positions = (place[3] + part * TILE + lax.broadcasted_iota(jnp.int32, (1, TILE), 1)).astype(F32)
    change = jnp.zeros((256, TILE), F32)
    placed = jnp.zeros((256, TILE), F32)
    size = 512
    for c in range(STEPS * BLOCK // size):
        at = slice(size * c, size * c + size)
        s, first = (size * c) // BLOCK, (size * c) % BLOCK // 32
        block = slice(first, first + size // 32), slice(32 * s, 32 * s + 32), slice(0, 256)
        products = jnp.dot(near[block].reshape(size, 256), source_near, preferred_element_type=F32)
        products = products + jnp.dot(far[block].reshape(size, 256), source_far, preferred_element_type=F32)
        kern = jnp.exp2((2.0 * SCALE) * products - (SCALE * sq[at] + source_sq))
        here = jnp.where(local[at] == positions, 1.0, 0.0).astype(BF16)
        weights = delta[:, at]
        for part in split3(kern):
            change = change + jnp.dot(weights, part, preferred_element_type=F32)
        placed = placed + jnp.dot(weights, here, preferred_element_type=F32)
    for at, out in ((0, mine_ref), (128, theirs_ref)):
        moved = change[at : at + 40] + (change[at + 40 : at + 80] + change[at + 80 : at + 120])
        added = placed[at : at + 40] + (placed[at + 40 : at + 80] + placed[at + 80 : at + 120])
        out[0] = moved + RIDGE * added
        out[1] = added


def update(part, place, sources, across, near, far, delta, sq, local):
    whole = pl.BlockSpec(memory_space=pltpu.VMEM)
    return pl.pallas_call(
        functools.partial(update_kernel, part),
        grid=(1,),
        in_specs=[pl.BlockSpec(memory_space=pltpu.SMEM)]
        + [pl.BlockSpec((112, TILE), lambda i: (0, part))] * 3
        + [whole] * (len(across) + 5),
        out_specs=[whole] * 2,
        out_shape=[jax.ShapeDtypeStruct((2, 40, TILE), F32)] * 2,
        compiler_params=pltpu.CompilerParams(vmem_limit_bytes=40 << 20),
        name="update",
    )(place, *sources, *across, near, far, delta, sq, local)


def finish_kernel(place, residual, coefficients, mine0, mine1, got0, got1, res_out, coef_out):
    own = pl.program_id(0) == place[1]
    for i, (mine, got) in enumerate(((mine0, got0), (mine1, got1))):
        at = slice(TILE * i, TILE * i + TILE)
        value = jnp.where(own, mine[...], got[...])
        res_out[:, at] = residual[:, at] - value[0, :ROWS]
        coef_out[:, at] = coefficients[:, at] + value[1, :ROWS]


def finish(place, residual, coefficients, *parts):
    whole = pl.BlockSpec(memory_space=pltpu.VMEM)
    half = pl.BlockSpec((ROWS, residual.shape[1] // 2), lambda i: (0, i))
    return pl.pallas_call(
        finish_kernel,
        grid=(2,),
        in_specs=[pl.BlockSpec(memory_space=pltpu.SMEM), half, half] + [whole] * 4,
        out_specs=[half, half],
        out_shape=[jax.ShapeDtypeStruct(residual.shape, F32)] * 2,
        compiler_params=pltpu.CompilerParams(vmem_limit_bytes=40 << 20),
        name="finish",
    )(place, residual, coefficients, *parts)


def on_device(frames, residual, coefficients, block_index):
    rows = frames.shape[1]
    dp, feat = lax.axis_index("dp"), lax.axis_index("feat")
    h, c = feat // 2, feat % 2
    place = jnp.stack([h, c, dp * rows, dp * rows + c * (rows // 2)]).astype(jnp.int32)
    own_half = lax.dynamic_slice_in_dim(frames, c * (rows // 2), rows // 2, axis=1)
    other_half = lax.dynamic_slice_in_dim(frames, (1 - c) * (rows // 2), rows // 2, axis=1)
    beside = swap(other_half, 0, 1)
    size = rows // 8
    own = [own_half[:, :size], own_half[:, size : 2 * size], own_half[:, 2 * size :]]
    across = [swap(own[0], 1, 0)]

    held = pick(place, block_index, frames, residual)
    held = add(lax.all_to_all(held, "dp", 0, 0, axis_index_groups=PLANE, tiled=True))
    held, beside, across, own, other_half = lax.optimization_barrier((held, beside, across, own, other_half))
    held = lax.all_to_all(held, AXES, 0, 0, axis_index_groups=LINE, tiled=True)
    held, own, other_half = lax.optimization_barrier((held, own, other_half))
    across.append(swap(own[1], 1, 0))
    near = lax.all_to_all(mix(place, held), "dp", 0, 0, axis_index_groups=PLANE, tiled=True)
    near, across, own, other_half = lax.optimization_barrier((near, across, own, other_half))
    far = swap(near, 0, 1)
    across.append(swap(own[2], 1, 0))
    diagonal = swap(other_half, 1, 1)

    delta, sq, local = solve(near, far, block_index)
    sources = own_half, beside, diagonal
    mine0, theirs0 = update(0, place, sources, across[:2], near, far, delta, sq, local)
    near, mine0, theirs0 = lax.optimization_barrier((near, mine0, theirs0))
    got0 = swap(theirs0, 0, 1)
    mine1, theirs1 = update(1, place, sources, across[2:], near, far, delta, sq, local)
    got1 = swap(theirs1, 0, 1)
    return finish(place, residual, coefficients, mine0, mine1, got0, got1)


def solution(mesh):
    return jax.shard_map(
        on_device,
        mesh=mesh,
        in_specs=(P("feat", "dp"), P("feat", "dp"), P("feat", "dp"), P()),
        out_specs=(P("feat", "dp"), P("feat", "dp")),
        check_vma=False,
    )
```
